512 devices in a mesh: dp: 16 (over y, x), shard: 32 (over z, core).
Axes of the slice: x: 4, y: 4, z: 16, core: 2. Of those that a mesh axis runs over, the one named last changes fastest.
Arguments:
- grad_parts: bfloat16 [16, 384, 256, 256], P('dp', 'shard'), may hold values from -4.5 to 4.5
- owner_list: int32 [384, 1], P('shard'), may hold values from 0 to 15; in each aligned block of 12 rows (0 to 11, 12 to 23, ...) at most 2 rows name the same one
- left_stats: float32 [16, 32, 2, 256, 256], P('dp', 'shard'), may hold values from -9 to 2560, as said below
- right_stats: float32 [16, 32, 2, 256, 256], P('dp', 'shard'), may hold values from -9 to 2560, as said below
Outputs:
- update: bfloat16 [384, 256, 256], P('shard')
- left_new: float32 [16, 32, 2, 256, 256], P('dp', 'shard')
- right_new: float32 [16, 32, 2, 256, 256], P('dp', 'shard')
The draws below stay inside these ranges and needn't reach their ends.
Inputs may be any that keep to these rules, and one draw needn't show every extreme that they name: `owner_list`: within each column (aligned blocks of 12 consecutive blocks) no owner index is named more than 2 times. `left_stats`: each matrix is symmetric positive definite. `right_stats`: each matrix is symmetric positive definite.
All inputs are finite; a program needn't handle non-finite values.
Results may differ from the reference program's by a relative error of at most 0.001.
Values may be sent and summed in bfloat16 or wider, within the bound.
A program may use at most 64 MiB of HBM per device.

```python
import math
import jax
import jax.numpy as jnp
import numpy as np
from jax import lax

BS = 256
CAP = 2
ITERS = 4
NBC = 12
NB = 384
N_DP = 16
N_SHARD = 32


def stat_matrix(key, lowest, highest):
    full_shape = (N_DP, N_SHARD, CAP, BS)
    diagonal = BS * jnp.exp(jax.random.uniform(key, full_shape, jnp.float32, math.log(lowest), math.log(highest)))
    uniform_part = jax.random.uniform(jax.random.fold_in(key, 1), full_shape + (BS,), jnp.float32, -1.0, 1.0)
    symmetric = 0.5 * (uniform_part + jnp.swapaxes(uniform_part, -1, -2))
    off_bound = jnp.minimum(diagonal[..., :, None], diagonal[..., None, :]) * (0.9 / BS)
    identity = jnp.eye(BS, dtype=jnp.float32)
    return symmetric * off_bound * (1.0 - identity) + diagonal[..., :, None] * identity


def draw_grad_parts(key, part):
    key = jax.random.fold_in(key, 11)
    full_shape = (N_DP, NB, BS, BS)
    block_ramp = 3.0 ** (jnp.arange(NB, dtype=jnp.float32) / (NB - 1))
    values = jnp.clip(jax.random.normal(key, full_shape, jnp.float32), -6.0, 6.0)
    return (0.25 * values * block_ramp[None, :, None, None]).astype(jnp.bfloat16)


def draw_left_stats(key, part):
    key = jax.random.fold_in(key, 21)
    return stat_matrix(key, 0.3, 3.0)


def draw_right_stats(key, part):
    key = jax.random.fold_in(key, 31)
    return stat_matrix(key, 0.3, 3.0)


def shared_out(key, own, number, rows, count, top, bound, slope):
    ranking = jax.random.permutation(key, count)
    heavy_load, ordinary = portions_of(count, rows * top, bound, slope, True), portions_of(count, rows * top, bound, slope, False)
    places = jnp.arange(count)

    def named(tallies, offset_by):
        used = int((tallies > 0).sum())
        fixed = max(1, used // 4)
        moved = fixed + (places - fixed + offset_by * (used - fixed)) % max(1, count - fixed)
        return jnp.zeros((count,), jnp.int32).at[ranking[jnp.where(places < fixed, places, moved)]].set(jnp.asarray(tallies, jnp.int32))

    tallies = jnp.where(number % 4 == 0, named(heavy_load, number // 4), named(ordinary, number - number // 4 - 1))
    mixed = jax.random.permutation(jax.random.fold_in(own, 3), count)
    giver, taker = mixed[0:count // 2 * 2:2], mixed[1:count // 2 * 2:2]
    margin = jnp.minimum(tallies[giver] - 1, bound - tallies[taker]) // 2
    margin = jnp.where((giver == ranking[0]) | (taker == ranking[0]) | (tallies[taker] == 0), 0, jnp.maximum(margin, 0))
    moved = jax.random.randint(jax.random.fold_in(own, 4), (count // 2,), 0, 1 << 20) % (margin + 1)
    tallies = tallies.at[giver].add(-moved).at[taker].add(moved)
    members = jnp.searchsorted(jnp.cumsum(tallies), jnp.arange(rows * top), side="right").astype(jnp.int32)
    listing = members.reshape(top, rows).T
    listing = listing[jax.random.permutation(jax.random.fold_in(own, 1), rows)]
    offset_by = jax.random.randint(jax.random.fold_in(own, 2), (rows, 1), 0, top)
    return jnp.take_along_axis(listing, (jnp.arange(top)[None, :] + offset_by) % top, axis=1)


def portions_of(amount, total, reach, skew, full):
    loads = [(1 << 20) // math.isqrt(rank ** skew) + 1 for rank in range(1, amount + 1)]
    largest = reach if full else min(reach, max(-(-total // amount), total * loads[0] // sum(loads)))
    least = 1 if total - largest >= amount - 1 else 0
    given, rest = [largest] + [least] * (amount - 1), total - largest - least * (amount - 1)
    while rest > 0:
        free = [i for i in range(1, amount) if given[i] < largest] or [i for i in range(1, amount) if given[i] < reach]
        pool, remaining = sum([loads[i] for i in free]), rest
        for i in free:
            extra = min(reach - given[i], max(1, remaining * loads[i] // pool), rest)
            given[i] = given[i] + extra
            rest = rest - extra
    return np.array(given)


def setup_inputs(seed: int = 0) -> dict:
    seeds = jax.random.split(jax.random.key(seed), 5)
    grad_parts = draw_grad_parts(jax.random.fold_in(seeds[4], 71), 0)
    owner_list_keys = jax.random.split(jax.random.fold_in(seeds[1], 1), NB // NBC)
    owner_list_turns = jax.random.permutation(jax.random.fold_in(seeds[1], 3), NB // NBC)
    owner_list = jax.vmap(lambda own, number: shared_out(jax.random.fold_in(seeds[1], 2), own, number, NBC, N_DP, 1, CAP, 2))(owner_list_keys, owner_list_turns).reshape((NB, 1))
    left_stats = draw_left_stats(jax.random.fold_in(seeds[4], 71), 0)
    right_stats = draw_right_stats(jax.random.fold_in(seeds[4], 71), 0)
    return {"grad_parts": grad_parts, "owner_list": owner_list, "left_stats": left_stats, "right_stats": right_stats}


DECAY_RATE = 0.9
ROOT_ORDER = 4.0
RIDGE_SCALE = 0.01

def product(left_mat, right_mat):
    return jnp.dot(left_mat, right_mat, precision=lax.Precision.HIGHEST, preferred_element_type=jnp.float32)

def slot_ranks(owner_column):
    block_count = owner_column.shape[0]
    same_owner = owner_column[:, None] == owner_column[None, :]
    earlier = jnp.arange(block_count)[:, None] > jnp.arange(block_count)[None, :]
    return lax.optimization_barrier(jnp.sum((same_owner & earlier).astype(jnp.int32), axis=1)).astype(jnp.int32)

def inverse_root(statistic):
    block_width = statistic.shape[0]
    identity = jnp.eye(block_width, dtype=jnp.float32)
    shifted = statistic + RIDGE_SCALE * jnp.trace(statistic) / block_width * identity
    norm_scale = (ROOT_ORDER + 1.0) / (2.0 * jnp.sqrt(jnp.sum(shifted * shifted) + 1e-06))
    root_mat = norm_scale ** (1.0 / ROOT_ORDER) * identity
    power_mat = norm_scale * shifted
    for iteration in range(ITERS):
        factor = ((ROOT_ORDER + 1.0) * identity - power_mat) / ROOT_ORDER
        root_mat = product(root_mat, factor)
        square = product(factor, factor)
        power_mat = product(product(square, square), power_mat)
    return root_mat

def reference(grad_parts, owner_list, left_stats, right_stats):
    grads = lax.optimization_barrier(jnp.sum(grad_parts.astype(jnp.float32), axis=0))
    owners = owner_list[:, 0].astype(jnp.int32)
    slot_rank = jax.vmap(slot_ranks)(owners.reshape(N_SHARD, NBC)).reshape(-1).astype(jnp.int32)
    column_ids = (jnp.arange(NB) // NBC).astype(jnp.int32)

    def one_block(block_index):
        gradient = grads[block_index]
        owner = owners[block_index]
        column = column_ids[block_index]
        slot = slot_rank[block_index]
        left_next = DECAY_RATE * left_stats[owner, column, slot] + (1.0 - DECAY_RATE) * product(gradient, gradient.T)
        right_next = DECAY_RATE * right_stats[owner, column, slot] + (1.0 - DECAY_RATE) * product(gradient.T, gradient)
        direction = product(product(inverse_root(left_next), gradient), inverse_root(right_next))
        graft_ratio = jnp.sqrt(jnp.mean(gradient * gradient)) / jnp.sqrt(jnp.mean(direction * direction) + 1e-06)
        return (left_next, right_next, (direction * graft_ratio).astype(jnp.bfloat16))
    lefts, rights, update = lax.map(one_block, jnp.arange(NB, dtype=jnp.int32))
    left_new = (DECAY_RATE * left_stats).at[owners, column_ids, slot_rank].set(lefts)
    right_new = (DECAY_RATE * right_stats).at[owners, column_ids, slot_rank].set(rights)
    return (update, left_new, right_new)
```

```python
import functools

import jax
import jax.numpy as jnp
from jax import lax
from jax.experimental import pallas as pl
from jax.experimental.pallas import tpu as pltpu
from jax.sharding import PartitionSpec as P

ITERS = 4
DECAY = 0.9
RIDGE = 0.01
ROWS = 16
HALF = 6
BF16, F32 = jnp.bfloat16, jnp.float32
MESH = pl.DeviceIdType.MESH
A, B0, B1, C0, C1, D0, D1 = range(7)


def split(value):
    high = value.astype(BF16)
    return high, (value - high.astype(F32)).astype(BF16)


def product(first, second):
    (ah, al), (bh, bl) = first, second
    return jnp.dot(
        jnp.concatenate([ah, ah, al], axis=1),
        jnp.concatenate([bh, bl, bh], axis=0),
        preferred_element_type=F32,
    )


def total(value):
    return jnp.sum(jnp.sum(value, axis=0, keepdims=True), axis=1, keepdims=True)


def ranks_of(owners):
    ranks = []
    for b, owner in enumerate(owners):
        rank = jnp.int32(0)
        for other in owners[:b]:
            rank = rank + jnp.where(other == owner, 1, 0)
        ranks.append(rank)
    firsts = sum(jnp.where(rank == 0, 1, 0) for rank in ranks)
    places, first, second = [], jnp.int32(0), firsts
    for rank in ranks:
        places.append(jnp.where(rank == 0, first, second))
        first = first + jnp.where(rank == 0, 1, 0)
        second = second + jnp.where(rank == 0, 0, 1)
    return ranks, places


def chosen(tests, values):
    return sum(jnp.where(test, value, 0) for test, value in zip(tests, values))


class Root:
    def __init__(self, statistic, eye):
        width = statistic.shape[0]
        shift = total(jnp.where(eye, statistic, 0.0)) * (RIDGE / width)
        shifted = statistic + jnp.where(eye, shift, 0.0)
        scale = 2.5 / jnp.sqrt(total(shifted * shifted) + 1e-06)
        self.eye = eye
        self.gain = jnp.sqrt(jnp.sqrt(scale))
        self.power = scale * shifted
        self.next_factor()

    def next_factor(self):
        self.factor = split(jnp.where(self.eye, 1.25, 0.0) - 0.25 * self.power)

    def advance(self):
        square = split(product(self.factor, self.factor))
        fourth = split(product(square, square))
        self.power = product(fourth, split(self.power))
        self.next_factor()


def kernel(
    side, own_ref, g_ref, ls_ref, rs_ref, upd_ref, ln_ref, rn_ref,
    parts, acc, picked0, picked1, grad0, grad1, left, right, left_out, right_out,
    ready0, ready1, home0, home1, gather0, gather1,
    owner_at, slot_at, block_at, send, recv, local,
):
    n = side * side
    blocks = own_ref.shape[0]
    me = lax.axis_index("dp")
    row, col = me // side, me % side

    def peer(k):
        return ((row + k // side) % side) * side + (col + k % side) % side

    barrier = pltpu.get_barrier_semaphore()

    @pl.loop(1, n)
    def _(k):
        pl.semaphore_signal(barrier, inc=1, device_id={"dp": peer(k)}, device_id_type=MESH)

    pl.semaphore_wait(barrier, n - 1)

    def copy(stage, k, src, dst):
        return pltpu.make_async_remote_copy(
            src_ref=src, dst_ref=dst, send_sem=send.at[stage, k], recv_sem=recv.at[stage, k],
            device_id={"dp": peer(k)}, device_id_type=MESH,
        )

    def part_copy(k):
        return copy(A, k, g_ref.at[:, peer(k)], parts.at[k])

    def slot_copy(slot, k):
        return copy((B0, B1)[slot], k, (picked0, picked1)[slot].at[k], (grad0, grad1)[slot].at[me])

    def home_copy(slot, k):
        return copy(
            (C0, C1)[slot], k, (ready0, ready1)[slot].at[peer(k)], (home0, home1)[slot].at[me]
        )

    def gather_copy(half, k):
        return copy(
            (D0, D1)[half], k, (gather0, gather1)[half], upd_ref.at[pl.ds(half * HALF, HALF), me]
        )

    @pl.loop(1, n)
    def _(k):
        part_copy(k).start()

    mine = pltpu.make_async_copy(g_ref.at[:, me], parts.at[0], local.at[0])
    mine.start()
    stats = [
        pltpu.make_async_copy(ls_ref, left, local.at[1]),
        pltpu.make_async_copy(rs_ref, right, local.at[2]),
    ]
    for each in stats:
        each.start()

    owners = [own_ref[b] for b in range(blocks)]
    ranks, places = ranks_of(owners)

    @pl.loop(0, n)
    def _(k):
        to = peer(k)
        for slot in range(2):
            tests = [(o == to) & (r == slot) for o, r in zip(owners, ranks)]
            block_at[slot, k] = chosen(tests, range(blocks))

    @pl.loop(0, blocks)
    def _(p):
        tests = [place == p for place in places]
        owner_at[p] = chosen(tests, owners)
        slot_at[p] = chosen(tests, ranks)

    used = [
        chosen([(o == me) & (r == slot) for o, r in zip(owners, ranks)], [1] * blocks) > 0
        for slot in range(2)
    ]

    mine.wait()
    acc[...] = parts[0].astype(F32)

    @pl.loop(1, n)
    def _(k):
        part_copy(k).wait_recv()
        acc[...] += parts[k].astype(F32)

    for slot in range(2):
        grad, picked = (grad0, grad1)[slot], (picked0, picked1)[slot]

        @pl.loop(1, n)
        def _(k):
            picked[k] = acc[block_at[slot, k]]
            slot_copy(slot, k).start()

        grad[me] = acc[block_at[slot, 0]]

    for each in stats:
        each.wait()

    def gather_half(half):
        @pl.loop(1, n)
        def _(k):
            home_copy(half, k).wait_recv()

        for p in range(HALF):
            at = half * HALF + p
            if half == 0:
                gather0[p] = home0[owner_at[at]]
            else:
                gather1[p] = jnp.where(slot_at[at] == 0, home0[owner_at[at]], home1[owner_at[at]])

        @pl.loop(1, n)
        def _(k):
            gather_copy(half, k).start()

    for slot in range(2):
        grad, ready, home = (grad0, grad1)[slot], (ready0, ready1)[slot], (home0, home1)[slot]

        @pl.loop(1, n)
        def _(k):
            slot_copy(slot, k).wait_recv()

        width = left.shape[1]
        value = jnp.where(used[slot], grad[...].reshape(width, width), 0.0)
        eye = lax.broadcasted_iota(jnp.int32, (width, width), 0) == lax.broadcasted_iota(
            jnp.int32, (width, width), 1
        )
        plain, turned = split(value), split(value.T)
        left_new = DECAY * left[slot] + (1.0 - DECAY) * product(plain, turned)
        right_new = DECAY * right[slot] + (1.0 - DECAY) * product(turned, plain)
        left_out[slot] = left_new
        right_out[slot] = right_new
        first, second = Root(left_new, eye), Root(right_new, eye)
        moved = product(split(product(first.factor, plain)), second.factor)
        for step in range(1, ITERS):
            first.advance()
            second.advance()
            if slot == 1 and step == 1:
                gather_half(0)
            moved = product(split(product(first.factor, split(moved))), second.factor)
        direction = (first.gain * second.gain) * moved
        count = 1.0 / (width * width)
        ratio = jnp.sqrt(total(value * value) * count) / jnp.sqrt(
            total(direction * direction) * count + 1e-06
        )
        ready[...] = (direction * ratio).astype(BF16).reshape(ready.shape)

        @pl.loop(1, n)
        def _(k):
            home_copy(slot, k).start()

        home[me] = ready[me]

    results = [
        pltpu.make_async_copy(left_out, ln_ref, local.at[3]),
        pltpu.make_async_copy(right_out, rn_ref, local.at[4]),
        pltpu.make_async_copy(gather0, upd_ref.at[pl.ds(0, HALF), me], local.at[5]),
        pltpu.make_async_copy(gather1, upd_ref.at[pl.ds(HALF, HALF), me], local.at[6]),
    ]
    for each in results[:3]:
        each.start()
    gather_half(1)
    results[3].start()

    @pl.loop(1, n)
    def _(k):
        part_copy(k).wait_send()
        for slot in range(2):
            slot_copy(slot, k).wait_send()
            home_copy(slot, k).wait_send()

    for each in results:
        each.wait()

    @pl.loop(1, n)
    def _(k):
        for half in range(2):
            gather_copy(half, k).wait()


def order_kernel(own_ref, upd_ref, ln_ref, rn_ref, out_ref, lo_ref, ro_ref, sem):
    blocks = own_ref.shape[0]
    _, places = ranks_of([own_ref[b] for b in range(blocks)])
    copies = [
        pltpu.make_async_copy(ln_ref, lo_ref, sem.at[blocks]),
        pltpu.make_async_copy(rn_ref, ro_ref, sem.at[blocks + 1]),
    ]
    copies += [
        pltpu.make_async_copy(upd_ref.at[places[b]], out_ref.at[b], sem.at[b])
        for b in range(blocks)
    ]
    for each in copies:
        each.start()
    for each in copies:
        each.wait()


def local(side, grad_parts, owner_list, left_stats, right_stats):
    n = side * side
    _, blocks, width, _ = grad_parts.shape
    owners = owner_list[:, 0]
    tiles = (blocks, n, ROWS, width)
    pair = (2, width, width)
    vmem = pltpu.VMEM
    anywhere = pl.BlockSpec(memory_space=pl.ANY)
    scalars = pl.BlockSpec(memory_space=pltpu.SMEM)
    piece = (n, ROWS, width)
    shapes = (
        jax.ShapeDtypeStruct(tiles, BF16),
        jax.ShapeDtypeStruct(pair, F32),
        jax.ShapeDtypeStruct(pair, F32),
    )
    update, left_new, right_new = pl.pallas_call(
        functools.partial(kernel, side),
        out_shape=shapes,
        in_specs=[scalars] + [anywhere] * 3,
        out_specs=(anywhere,) * 3,
        scratch_shapes=[
            vmem((n, blocks, ROWS, width), BF16),
            vmem((blocks, ROWS, width), F32),
            vmem(piece, F32),
            vmem(piece, F32),
            vmem(piece, F32),
            vmem(piece, F32),
            vmem(pair, F32),
            vmem(pair, F32),
            vmem(pair, F32),
            vmem(pair, F32),
            vmem(piece, BF16),
            vmem(piece, BF16),
            vmem(piece, BF16),
            vmem(piece, BF16),
            vmem((HALF, ROWS, width), BF16),
            vmem((HALF, ROWS, width), BF16),
            pltpu.SMEM((blocks,), jnp.int32),
            pltpu.SMEM((blocks,), jnp.int32),
            pltpu.SMEM((2, n), jnp.int32),
            pltpu.SemaphoreType.DMA((7, n)),
            pltpu.SemaphoreType.DMA((7, n)),
            pltpu.SemaphoreType.DMA((7,)),
        ],
        compiler_params=pltpu.CompilerParams(
            collective_id=0, has_side_effects=True, vmem_limit_bytes=40 * 1024 * 1024
        ),
    )(
        owners,
        grad_parts.reshape(tiles),
        left_stats.reshape(pair),
        right_stats.reshape(pair),
    )
    update, left_new, right_new = pl.pallas_call(
        order_kernel,
        out_shape=shapes,
        in_specs=[scalars] + [anywhere] * 3,
        out_specs=(anywhere,) * 3,
        scratch_shapes=[pltpu.SemaphoreType.DMA((blocks + 2,))],
    )(owners, update, left_new, right_new)
    return (
        update.reshape(blocks, width, width),
        left_new.reshape(left_stats.shape),
        right_new.reshape(right_stats.shape),
    )


def solution(mesh):
    side = int(round(mesh.shape["dp"] ** 0.5))
    return jax.shard_map(
        functools.partial(local, side),
        mesh=mesh,
        in_specs=(
            P("dp", "shard", None, None),
            P("shard", None),
            P("dp", "shard", None, None, None),
            P("dp", "shard", None, None, None),
        ),
        out_specs=(
            P("shard", None, None),
            P("dp", "shard", None, None, None),
            P("dp", "shard", None, None, None),
        ),
        check_vma=False,
    )
```

```python
import functools

import jax
import jax.numpy as jnp
from jax import lax
from jax.experimental import pallas as pl
from jax.experimental.pallas import tpu as pltpu
from jax.sharding import PartitionSpec as P

ITERS = 4
DECAY = 0.9
RIDGE = 0.01
ROWS = 16
VMEM_BYTES = 56 * 1024 * 1024
HALF = 6
BF16, F32 = jnp.bfloat16, jnp.float32
MESH = pl.DeviceIdType.MESH
A, B0, B1, C0, C1, D0, D1 = range(7)


def split(value):
    high = value.astype(BF16)
    return high, (value - high.astype(F32)).astype(BF16)


def product(first, second):
    (ah, al), (bh, bl) = first, second
    return jnp.dot(
        jnp.concatenate([ah, ah, al], axis=1),
        jnp.concatenate([bh, bl, bh], axis=0),
        preferred_element_type=F32,
    )


def total(value):
    return jnp.sum(jnp.sum(value, axis=0, keepdims=True), axis=1, keepdims=True)


def ranks_of(owners):
    ranks = []
    for b, owner in enumerate(owners):
        rank = jnp.int32(0)
        for other in owners[:b]:
            rank = rank + jnp.where(other == owner, 1, 0)
        ranks.append(rank)
    firsts = sum(jnp.where(rank == 0, 1, 0) for rank in ranks)
    places, first, second = [], jnp.int32(0), firsts
    for rank in ranks:
        places.append(jnp.where(rank == 0, first, second))
        first = first + jnp.where(rank == 0, 1, 0)
        second = second + jnp.where(rank == 0, 0, 1)
    return ranks, places


def chosen(tests, values):
    return sum(jnp.where(test, value, 0) for test, value in zip(tests, values))


class Root:
    def __init__(self, statistic, eye):
        width = statistic.shape[0]
        shift = total(jnp.where(eye, statistic, 0.0)) * (RIDGE / width)
        shifted = statistic + jnp.where(eye, shift, 0.0)
        scale = 2.5 / jnp.sqrt(total(shifted * shifted) + 1e-06)
        self.eye = eye
        self.gain = jnp.sqrt(jnp.sqrt(scale))
        self.power = scale * shifted
        self.next_factor()

    def next_factor(self):
        self.factor = split(jnp.where(self.eye, 1.25, 0.0) - 0.25 * self.power)

    def advance(self):
        square = split(product(self.factor, self.factor))
        fourth = split(product(square, square))
        self.power = product(fourth, split(self.power))
        self.next_factor()


def kernel(
    side, own_ref, g_ref, ls_ref, rs_ref, upd_ref, ln_ref, rn_ref,
    parts, acc, picked0, picked1, grad0, grad1, left, right, left_out, right_out,
    ready0, ready1, home0, home1, gather0, gather1,
    owner_at, slot_at, block_at, send, recv, local,
):
    n = side * side
    blocks = own_ref.shape[0]
    me = lax.axis_index("dp")
    row, col = me // side, me % side

    def peer(k):
        return ((row + k // side) % side) * side + (col + k % side) % side

    barrier = pltpu.get_barrier_semaphore()

    @pl.loop(1, n)
    def _(k):
        pl.semaphore_signal(barrier, inc=1, device_id={"dp": peer(k)}, device_id_type=MESH)

    pl.semaphore_wait(barrier, n - 1)

    def copy(stage, k, src, dst):
        return pltpu.make_async_remote_copy(
            src_ref=src, dst_ref=dst, send_sem=send.at[stage, k], recv_sem=recv.at[stage, k],
            device_id={"dp": peer(k)}, device_id_type=MESH,
        )

    def part_copy(k):
        return copy(A, k, g_ref.at[:, peer(k)], parts.at[k])

    def slot_copy(slot, k):
        return copy((B0, B1)[slot], k, (picked0, picked1)[slot].at[k], (grad0, grad1)[slot].at[me])

    def home_copy(slot, k):
        return copy(
            (C0, C1)[slot], k, (ready0, ready1)[slot].at[peer(k)], (home0, home1)[slot].at[me]
        )

    def gather_copy(half, k):
        return copy(
            (D0, D1)[half], k, (gather0, gather1)[half], upd_ref.at[pl.ds(half * HALF, HALF), me]
        )

    @pl.loop(1, n)
    def _(k):
        part_copy(k).start()

    mine = pltpu.make_async_copy(g_ref.at[:, me], parts.at[0], local.at[0])
    mine.start()
    stats = [
        pltpu.make_async_copy(ls_ref, left, local.at[1]),
        pltpu.make_async_copy(rs_ref, right, local.at[2]),
    ]
    for each in stats:
        each.start()

    owners = [own_ref[b] for b in range(blocks)]
    ranks, places = ranks_of(owners)

    @pl.loop(0, n)
    def _(k):
        to = peer(k)
        for slot in range(2):
            tests = [(o == to) & (r == slot) for o, r in zip(owners, ranks)]
            block_at[slot, k] = chosen(tests, range(blocks))

    @pl.loop(0, blocks)
    def _(p):
        tests = [place == p for place in places]
        owner_at[p] = chosen(tests, owners)
        slot_at[p] = chosen(tests, ranks)

    used = [
        chosen([(o == me) & (r == slot) for o, r in zip(owners, ranks)], [1] * blocks) > 0
        for slot in range(2)
    ]

    mine.wait()
    acc[...] = parts[0].astype(F32)

    @pl.loop(1, n)
    def _(k):
        part_copy(k).wait_recv()
        acc[...] += parts[k].astype(F32)

    for slot in range(2):
        grad, picked = (grad0, grad1)[slot], (picked0, picked1)[slot]

        @pl.loop(1, n)
        def _(k):
            picked[k] = acc[block_at[slot, k]]
            slot_copy(slot, k).start()

        grad[me] = acc[block_at[slot, 0]]

    for each in stats:
        each.wait()

    def gather_half(half):
        @pl.loop(1, n)
        def _(k):
            home_copy(half, k).wait_recv()

        for p in range(HALF):
            at = half * HALF + p
            if half == 0:
                gather0[p] = home0[owner_at[at]]
            else:
                gather1[p] = jnp.where(slot_at[at] == 0, home0[owner_at[at]], home1[owner_at[at]])

        @pl.loop(1, n)
        def _(k):
            gather_copy(half, k).start()

    for slot in range(2):
        grad, ready, home = (grad0, grad1)[slot], (ready0, ready1)[slot], (home0, home1)[slot]

        @pl.loop(1, n)
        def _(k):
            slot_copy(slot, k).wait_recv()

        width = left.shape[1]
        value = jnp.where(used[slot], grad[...].reshape(width, width), 0.0)
        eye = lax.broadcasted_iota(jnp.int32, (width, width), 0) == lax.broadcasted_iota(
            jnp.int32, (width, width), 1
        )
        plain, turned = split(value), split(value.T)
        left_new = DECAY * left[slot] + (1.0 - DECAY) * product(plain, turned)
        right_new = DECAY * right[slot] + (1.0 - DECAY) * product(turned, plain)
        left_out[slot] = left_new
        right_out[slot] = right_new
        first, second = Root(left_new, eye), Root(right_new, eye)
        moved = product(split(product(first.factor, plain)), second.factor)
        for step in range(1, ITERS):
            first.advance()
            second.advance()
            if slot == 1 and step == 1:
                gather_half(0)
            moved = product(split(product(first.factor, split(moved))), second.factor)
        direction = (first.gain * second.gain) * moved
        count = 1.0 / (width * width)
        ratio = jnp.sqrt(total(value * value) * count) / jnp.sqrt(
            total(direction * direction) * count + 1e-06
        )
        ready[...] = (direction * ratio).astype(BF16).reshape(ready.shape)

        @pl.loop(1, n)
        def _(k):
            home_copy(slot, k).start()

        home[me] = ready[me]

    results = [
        pltpu.make_async_copy(left_out, ln_ref, local.at[3]),
        pltpu.make_async_copy(right_out, rn_ref, local.at[4]),
        pltpu.make_async_copy(gather0, upd_ref.at[pl.ds(0, HALF), me], local.at[5]),
        pltpu.make_async_copy(gather1, upd_ref.at[pl.ds(HALF, HALF), me], local.at[6]),
    ]
    for each in results[:3]:
        each.start()
    gather_half(1)
    results[3].start()

    @pl.loop(1, n)
    def _(k):
        part_copy(k).wait_send()
        for slot in range(2):
            slot_copy(slot, k).wait_send()
            home_copy(slot, k).wait_send()

    for each in results:
        each.wait()

    @pl.loop(1, n)
    def _(k):
        for half in range(2):
            gather_copy(half, k).wait()


def order_kernel(
    own_ref, upd_ref, ln_ref, rn_ref, out_ref, lo_ref, ro_ref, upd, left, right, into, out
):
    blocks = own_ref.shape[0]
    _, places = ranks_of([own_ref[b] for b in range(blocks)])
    moves = [
        (upd_ref.at[places[b]], upd.at[b], out_ref.at[b]) for b in range(blocks)
    ] + [(ln_ref, left, lo_ref), (rn_ref, right, ro_ref)]
    reads = [pltpu.make_async_copy(m[0], m[1], into.at[i]) for i, m in enumerate(moves)]
    writes = [pltpu.make_async_copy(m[1], m[2], out.at[i]) for i, m in enumerate(moves)]
    for read in reads:
        read.start()
    for read, write in zip(reads, writes):
        read.wait()
        write.start()
    for write in writes:
        write.wait()


def local(side, grad_parts, owner_list, left_stats, right_stats):
    n = side * side
    _, blocks, width, _ = grad_parts.shape
    owners = owner_list[:, 0]
    tiles = (blocks, n, ROWS, width)
    pair = (2, width, width)
    vmem = pltpu.VMEM
    anywhere = pl.BlockSpec(memory_space=pl.ANY)
    scalars = pl.BlockSpec(memory_space=pltpu.SMEM)
    piece = (n, ROWS, width)
    shapes = (
        jax.ShapeDtypeStruct(tiles, BF16),
        jax.ShapeDtypeStruct(pair, F32),
        jax.ShapeDtypeStruct(pair, F32),
    )
    update, left_new, right_new = pl.pallas_call(
        functools.partial(kernel, side),
        out_shape=shapes,
        in_specs=[scalars] + [pl.BlockSpec(memory_space=pltpu.HBM)] * 3,
        out_specs=(anywhere,) * 3,
        scratch_shapes=[
            vmem((n, blocks, ROWS, width), BF16),
            vmem((blocks, ROWS, width), F32),
            vmem(piece, F32),
            vmem(piece, F32),
            vmem(piece, F32),
            vmem(piece, F32),
            vmem(pair, F32),
            vmem(pair, F32),
            vmem(pair, F32),
            vmem(pair, F32),
            vmem(piece, BF16),
            vmem(piece, BF16),
            vmem(piece, BF16),
            vmem(piece, BF16),
            vmem((HALF, ROWS, width), BF16),
            vmem((HALF, ROWS, width), BF16),
            pltpu.SMEM((blocks,), jnp.int32),
            pltpu.SMEM((blocks,), jnp.int32),
            pltpu.SMEM((2, n), jnp.int32),
            pltpu.SemaphoreType.DMA((7, n)),
            pltpu.SemaphoreType.DMA((7, n)),
            pltpu.SemaphoreType.DMA((7,)),
        ],
        compiler_params=pltpu.CompilerParams(
            collective_id=0, has_side_effects=True, vmem_limit_bytes=VMEM_BYTES
        ),
    )(
        owners,
        grad_parts.reshape(tiles),
        left_stats.reshape(pair),
        right_stats.reshape(pair),
    )
    update, left_new, right_new = pl.pallas_call(
        order_kernel,
        out_shape=shapes,
        in_specs=[scalars] + [anywhere] * 3,
        out_specs=(anywhere,) * 3,
        scratch_shapes=[
            vmem(tiles, BF16),
            vmem(pair, F32),
            vmem(pair, F32),
            pltpu.SemaphoreType.DMA((blocks + 2,)),
            pltpu.SemaphoreType.DMA((blocks + 2,)),
        ],
        compiler_params=pltpu.CompilerParams(vmem_limit_bytes=VMEM_BYTES),
    )(owners, update, left_new, right_new)
    return (
        update.reshape(blocks, width, width),
        left_new.reshape(left_stats.shape),
        right_new.reshape(right_stats.shape),
    )


def solution(mesh):
    side = int(round(mesh.shape["dp"] ** 0.5))
    return jax.shard_map(
        functools.partial(local, side),
        mesh=mesh,
        in_specs=(
            P("dp", "shard", None, None),
            P("shard", None),
            P("dp", "shard", None, None, None),
            P("dp", "shard", None, None, None),
        ),
        out_specs=(
            P("shard", None, None),
            P("dp", "shard", None, None, None),
            P("dp", "shard", None, None, None),
        ),
        check_vma=False,
    )
```

```python
import functools

import jax
import jax.numpy as jnp
from jax import lax
from jax.experimental import pallas as pl
from jax.experimental.pallas import tpu as pltpu
from jax.sharding import PartitionSpec as P

ITERS = 4
DECAY = 0.9
RIDGE = 0.01
ROWS = 16
VMEM_BYTES = 56 * 1024 * 1024
HALF = 6
BF16, F32 = jnp.bfloat16, jnp.float32
MESH = pl.DeviceIdType.MESH
A, B0, B1, C0, C1, D0, D1 = range(7)


def split(value):
    high = value.astype(BF16)
    return high, (value - high.astype(F32)).astype(BF16)


def product(first, second):
    (ah, al), (bh, bl) = first, second
    return jnp.dot(
        jnp.concatenate([ah, ah, al], axis=1),
        jnp.concatenate([bh, bl, bh], axis=0),
        preferred_element_type=F32,
    )


def total(value):
    return jnp.sum(jnp.sum(value, axis=0, keepdims=True), axis=1, keepdims=True)


def ranks_of(owners):
    ranks = []
    for b, owner in enumerate(owners):
        rank = jnp.int32(0)
        for other in owners[:b]:
            rank = rank + jnp.where(other == owner, 1, 0)
        ranks.append(rank)
    firsts = sum(jnp.where(rank == 0, 1, 0) for rank in ranks)
    places, first, second = [], jnp.int32(0), firsts
    for rank in ranks:
        places.append(jnp.where(rank == 0, first, second))
        first = first + jnp.where(rank == 0, 1, 0)
        second = second + jnp.where(rank == 0, 0, 1)
    return ranks, places


def chosen(tests, values):
    return sum(jnp.where(test, value, 0) for test, value in zip(tests, values))


class Root:
    def __init__(self, statistic, eye):
        width = statistic.shape[0]
        shift = total(jnp.where(eye, statistic, 0.0)) * (RIDGE / width)
        shifted = statistic + jnp.where(eye, shift, 0.0)
        scale = 2.5 / jnp.sqrt(total(shifted * shifted) + 1e-06)
        self.eye = eye
        self.gain = jnp.sqrt(jnp.sqrt(scale))
        self.power = scale * shifted
        self.next_factor()

    def next_factor(self):
        self.factor = split(jnp.where(self.eye, 1.25, 0.0) - 0.25 * self.power)

    def advance(self):
        square = split(product(self.factor, self.factor))
        fourth = split(product(square, square))
        self.power = product(fourth, split(self.power))
        self.next_factor()


def kernel(
    side, own_ref, g_ref, ls_ref, rs_ref, upd_ref, ln_ref, rn_ref,
    parts, relay, sums, second, relay2, acc, picked0, picked1, grad0, grad1,
    left, right, left_out, right_out, ready0, ready1, home0, home1, gathered,
    owner_at, slot_at, block_at,
    send_a, recv_a, send_b, recv_b, send_d, recv_d, send, recv, local,
):
    n = side * side
    blocks = own_ref.shape[0]
    me = lax.axis_index("dp")
    row, col = me // side, me % side
    chunk = HALF // 2

    def peer(k):
        return ((row + k // side) % side) * side + (col + k % side) % side

    def place(kind, du, dv):
        dy, dx = (dv, du) if kind == 0 else (du, dv)
        return ((row + dy + side) % side) * side + (col + dx + side) % side

    def line(kind, du, dv):
        at = [(c + d + side) % side for c, d in zip((col, row) if kind == 0 else (row, col), (du, dv))]
        return at

    barrier = pltpu.get_barrier_semaphore()

    @pl.loop(1, n)
    def _(k):
        pl.semaphore_signal(barrier, inc=1, device_id={"dp": peer(k)}, device_id_type=MESH)

    pl.semaphore_wait(barrier, n - 1)

    def remote(src, dst, sent, landed, to):
        return pltpu.make_async_remote_copy(
            src_ref=src, dst_ref=dst, send_sem=sent, recv_sem=landed,
            device_id={"dp": to}, device_id_type=MESH,
        )

    started = []

    def begin(copy):
        copy.start()
        started.append(copy)

    def raw_copy(kind, j, what, way):
        step = 1 - 2 * way
        rows = pl.ds(way * (side // 2), side // 2)
        source = g_ref.at[pl.ds(kind * HALF + j * chunk, chunk)]
        u = line(kind, 2 if what == 0 else step, 0)[0]
        if what == 0:
            src, dst = source.at[:, u, rows], relay.at[kind, j, way]
        elif what == 1:
            src, dst = source.at[:, u], parts.at[kind, j, way]
        else:
            src, dst = relay.at[kind, j, way], parts.at[kind, j, 2, :, rows]
        at = (kind, j, what, way)
        return remote(src, dst, send_a.at[at], recv_a.at[at], place(kind, step, 0))

    def sum_copy(kind, j, what, way):
        step = 1 - 2 * way
        rows = pl.ds(way * (ROWS // 2), ROWS // 2)
        v = line(kind, 0, 2 if what == 0 else step)[1]
        if what == 0:
            src, dst = sums.at[kind, j, v, :, rows], relay2.at[kind, j, way]
        elif what == 1:
            src, dst = sums.at[kind, j, v], second.at[kind, j, way]
        else:
            src, dst = relay2.at[kind, j, way], second.at[kind, j, 2, :, rows]
        at = (kind, j, what, way)
        return remote(src, dst, send_b.at[at], recv_b.at[at], place(kind, 0, step))

    def direct(stage, k, src, dst):
        return remote(src, dst, send.at[stage, k], recv.at[stage, k], peer(k))

    def slot_copy(slot, k):
        return direct(slot, k, (picked0, picked1)[slot].at[k], (grad0, grad1)[slot].at[me])

    def home_copy(slot, k):
        return direct(
            2 + slot, k, (ready0, ready1)[slot].at[peer(k)], (home0, home1)[slot].at[me]
        )

    kinds, ways = range(2), range(2)
    for j in range(2):
        for what in range(2):
            for way in ways:
                for kind in kinds:
                    begin(raw_copy(kind, j, what, way))
    mine = {}
    for j in range(2):
        for kind in kinds:
            mine[kind, j] = pltpu.make_async_copy(
                g_ref.at[pl.ds(kind * HALF + j * chunk, chunk), line(kind, 0, 0)[0]],
                parts.at[kind, j, 3],
                local.at[4 + 2 * kind + j],
            )
            mine[kind, j].start()
    stats = [
        pltpu.make_async_copy(ls_ref, left, local.at[0]),
        pltpu.make_async_copy(rs_ref, right, local.at[1]),
    ]
    for each in stats:
        each.start()

    owners = [own_ref[b] for b in range(blocks)]
    ranks, places = ranks_of(owners)

    @pl.loop(0, n)
    def _(k):
        to = peer(k)
        for slot in range(2):
            tests = [(o == to) & (r == slot) for o, r in zip(owners, ranks)]
            block_at[slot, k] = chosen(tests, range(blocks))

    @pl.loop(0, blocks)
    def _(p):
        tests = [at == p for at in places]
        owner_at[p] = chosen(tests, owners)
        slot_at[p] = chosen(tests, ranks)

    def mine_in(slot, first, last):
        tests = [(o == me) & (r == slot) for o, r in zip(owners[first:last], ranks[first:last])]
        return chosen(tests, [1] * (last - first)) > 0

    for j in range(2):
        for way in ways:
            for kind in kinds:
                raw_copy(kind, j, 0, way).wait_recv()
                begin(raw_copy(kind, j, 2, way))
    for j in range(2):
        for kind in kinds:
            for way in ways:
                raw_copy(kind, j, 1, way).wait_recv()
                raw_copy(kind, j, 2, way).wait_recv()
            mine[kind, j].wait()

            @pl.loop(0, side)
            def _(v):
                sums[kind, j, v] = sum(parts[kind, j, i, :, v].astype(F32) for i in range(side))

            for what in range(2):
                for way in ways:
                    begin(sum_copy(kind, j, what, way))
        for way in ways:
            for kind in kinds:
                sum_copy(kind, j, 0, way).wait_recv()
                begin(sum_copy(kind, j, 2, way))
    for j in range(2):
        for kind in kinds:
            for way in ways:
                sum_copy(kind, j, 1, way).wait_recv()
                sum_copy(kind, j, 2, way).wait_recv()
            v = line(kind, 0, 0)[1]
            acc[pl.ds(kind * HALF + j * chunk, chunk)] = sums[kind, j, v] + (
                second[kind, j, 0] + second[kind, j, 1] + second[kind, j, 2]
            )

    for slot in range(2):
        grad, picked = (grad0, grad1)[slot], (picked0, picked1)[slot]

        @pl.loop(1, n)
        def _(k):
            picked[k] = acc[block_at[slot, k]]
            slot_copy(slot, k).start()

        grad[me] = acc[block_at[slot, 0]]

    for each in stats:
        each.wait()

    def item_copy(half, kind, du, dv, over, cut=None):
        at = half * HALF + kind * chunk
        first, size = (0, chunk) if cut is None else cut
        ref = gathered.at[pl.ds(at + first, size), place(kind, du, dv)]
        seen = ((du - over[0]) % side, (dv - over[1]) % side)
        lane = seen[0] * side + seen[1]
        if cut is not None and first > 0:
            lane = 0
        sent = send_d.at[half, kind, (over[0] + 2 * over[1]) % 5 % 4, lane]
        return remote(ref, ref, sent, recv_d.at[half, kind, lane], place(kind, *over))

    def item_wait(half, kind, du, dv):
        cuts = [None]
        if dv == 0 and du % side == 2:
            cuts = [(0, 2), (2, 1)]
        for cut in cuts:
            at = half * HALF + kind * chunk
            first, size = (0, chunk) if cut is None else cut
            ref = gathered.at[pl.ds(at + first, size), place(kind, du, dv)]
            lane = (du % side) * side + dv % side
            if cut is not None and first > 0:
                lane = 0
            remote(
                ref, ref, send_d.at[half, kind, 0, 0], recv_d.at[half, kind, lane], place(kind, 0, 1)
            ).wait_recv()

    both = ((0, 1), (0, -1))

    def gather_start(half):
        @pl.loop(1, n)
        def _(k):
            home_copy(half, k).wait_recv()

        for p in range(HALF):
            at = half * HALF + p
            if half == 0:
                gathered[at, me] = home0[owner_at[at]]
            else:
                gathered[at, me] = jnp.where(
                    slot_at[at] == 0, home0[owner_at[at]], home1[owner_at[at]]
                )
        for kind in kinds:
            for over in ((1, 0), (-1, 0)):
                begin(item_copy(half, kind, 0, 0, over))
        for kind in kinds:
            for over in both:
                begin(item_copy(half, kind, 0, 0, over))

    def gather_near(half):
        for du in (-1, 1):
            for kind in kinds:
                item_wait(half, kind, du, 0)
                begin(item_copy(half, kind, du, 0, (-du, 0), (0, 2) if du < 0 else (2, 1)))
                for over in both:
                    begin(item_copy(half, kind, du, 0, over))

    def gather_far(half):
        for kind in kinds:
            item_wait(half, kind, 2, 0)
            for over in both:
                begin(item_copy(half, kind, 2, 0, over))

    def gather_relay(half, first):
        for du, dv in ((0, -1), (0, 1)) if first else ((-1, -1), (1, 1), (2, 1), (2, -1)):
            for kind in kinds:
                item_wait(half, kind, du, dv)
                if (du, dv) in ((0, -1), (-1, -1), (1, 1), (2, 1)):
                    begin(item_copy(half, kind, du, dv, (0, -dv)))

    def gather_end(half):
        for du, dv in ((-1, 1), (1, -1), (0, 2), (-1, 2), (1, 2), (2, 2)):
            for kind in kinds:
                item_wait(half, kind, du, dv)

    def finish(half):
        ref = pl.ds(half * HALF, HALF)
        copy = pltpu.make_async_copy(gathered.at[ref], upd_ref.at[ref], local.at[8 + half])
        copy.start()
        return copy

    results = []
    for slot in range(2):
        grad, ready, home = (grad0, grad1)[slot], (ready0, ready1)[slot], (home0, home1)[slot]

        @pl.loop(1, n)
        def _(k):
            slot_copy(slot, k).wait_recv()

        width = left.shape[1]
        across = jnp.stack([grad[(i % side) * side + i // side] for i in range(n)])
        value = jnp.where(
            mine_in(slot, 0, HALF),
            across,
            jnp.where(mine_in(slot, HALF, blocks), grad[...], 0.0),
        ).reshape(width, width)
        eye = lax.broadcasted_iota(jnp.int32, (width, width), 0) == lax.broadcasted_iota(
            jnp.int32, (width, width), 1
        )
        plain, turned = split(value), split(value.T)
        left_new = DECAY * left[slot] + (1.0 - DECAY) * product(plain, turned)
        right_new = DECAY * right[slot] + (1.0 - DECAY) * product(turned, plain)
        left_out[slot] = left_new
        right_out[slot] = right_new
        first, other = Root(left_new, eye), Root(right_new, eye)
        moved = product(split(product(first.factor, plain)), other.factor)
        for step in range(1, ITERS):
            first.advance()
            other.advance()
            if slot == 1:
                (gather_start, gather_near, gather_far)[step - 1](0)
            moved = product(split(product(first.factor, split(moved))), other.factor)
        direction = (first.gain * other.gain) * moved
        count = 1.0 / (width * width)
        ratio = jnp.sqrt(total(value * value) * count) / jnp.sqrt(
            total(direction * direction) * count + 1e-06
        )
        ready[...] = (direction * ratio).astype(BF16).reshape(ready.shape)

        @pl.loop(1, n)
        def _(k):
            home_copy(slot, k).start()

        home[me] = ready[me]

    results += [
        pltpu.make_async_copy(left_out, ln_ref, local.at[2]),
        pltpu.make_async_copy(right_out, rn_ref, local.at[3]),
    ]
    for each in results:
        each.start()
    gather_relay(0, True)
    gather_relay(0, False)
    gather_start(1)
    gather_near(1)
    gather_far(1)
    gather_end(0)
    results.append(finish(0))
    gather_relay(1, True)
    gather_relay(1, False)
    gather_end(1)
    results.append(finish(1))

    @pl.loop(1, n)
    def _(k):
        for slot in range(2):
            slot_copy(slot, k).wait_send()
            home_copy(slot, k).wait_send()

    for each in started:
        each.wait_send()
    for each in results:
        each.wait()


def order_kernel(
    own_ref, upd_ref, ln_ref, rn_ref, out_ref, lo_ref, ro_ref, upd, left, right, into, out
):
    blocks = own_ref.shape[0]
    _, places = ranks_of([own_ref[b] for b in range(blocks)])
    moves = [
        (upd_ref.at[places[b]], upd.at[b], out_ref.at[b]) for b in range(blocks)
    ] + [(ln_ref, left, lo_ref), (rn_ref, right, ro_ref)]
    reads = [pltpu.make_async_copy(m[0], m[1], into.at[i]) for i, m in enumerate(moves)]
    writes = [pltpu.make_async_copy(m[1], m[2], out.at[i]) for i, m in enumerate(moves)]
    for read in reads:
        read.start()
    for read, write in zip(reads, writes):
        read.wait()
        write.start()
    for write in writes:
        write.wait()


def local(side, grad_parts, owner_list, left_stats, right_stats):
    n = side * side
    _, blocks, width, _ = grad_parts.shape
    owners = owner_list[:, 0]
    tiles = (blocks, n, ROWS, width)
    chunk = HALF // 2
    pair = (2, width, width)
    vmem = pltpu.VMEM
    anywhere = pl.BlockSpec(memory_space=pl.ANY)
    scalars = pl.BlockSpec(memory_space=pltpu.SMEM)
    piece = (n, ROWS, width)
    shapes = (
        jax.ShapeDtypeStruct(tiles, BF16),
        jax.ShapeDtypeStruct(pair, F32),
        jax.ShapeDtypeStruct(pair, F32),
    )
    update, left_new, right_new = pl.pallas_call(
        functools.partial(kernel, side),
        out_shape=shapes,
        in_specs=[scalars] + [pl.BlockSpec(memory_space=pltpu.HBM)] * 3,
        out_specs=(anywhere,) * 3,
        scratch_shapes=[
            vmem((2, 2, side, chunk, side, ROWS, width), BF16),
            vmem((2, 2, 2, chunk, side // 2, ROWS, width), BF16),
            vmem((2, 2, side, chunk, ROWS, width), F32),
            vmem((2, 2, 3, chunk, ROWS, width), F32),
            vmem((2, 2, 2, chunk, ROWS // 2, width), F32),
            vmem((blocks, ROWS, width), F32),
            vmem(piece, F32),
            vmem(piece, F32),
            vmem(piece, F32),
            vmem(piece, F32),
            vmem(pair, F32),
            vmem(pair, F32),
            vmem(pair, F32),
            vmem(pair, F32),
            vmem(piece, BF16),
            vmem(piece, BF16),
            vmem(piece, BF16),
            vmem(piece, BF16),
            vmem(tiles, BF16),
            pltpu.SMEM((blocks,), jnp.int32),
            pltpu.SMEM((blocks,), jnp.int32),
            pltpu.SMEM((2, n), jnp.int32),
            pltpu.SemaphoreType.DMA((2, 2, 3, 2)),
            pltpu.SemaphoreType.DMA((2, 2, 3, 2)),
            pltpu.SemaphoreType.DMA((2, 2, 3, 2)),
            pltpu.SemaphoreType.DMA((2, 2, 3, 2)),
            pltpu.SemaphoreType.DMA((2, 2, 4, n)),
            pltpu.SemaphoreType.DMA((2, 2, n)),
            pltpu.SemaphoreType.DMA((4, n)),
            pltpu.SemaphoreType.DMA((4, n)),
            pltpu.SemaphoreType.DMA((10,)),
        ],
        compiler_params=pltpu.CompilerParams(
            collective_id=0, has_side_effects=True, vmem_limit_bytes=VMEM_BYTES
        ),
    )(
        owners,
        grad_parts.reshape(blocks, side, side, ROWS, width),
        left_stats.reshape(pair),
        right_stats.reshape(pair),
    )
    update, left_new, right_new = pl.pallas_call(
        order_kernel,
        out_shape=shapes,
        in_specs=[scalars] + [anywhere] * 3,
        out_specs=(anywhere,) * 3,
        scratch_shapes=[
            vmem(tiles, BF16),
            vmem(pair, F32),
            vmem(pair, F32),
            pltpu.SemaphoreType.DMA((blocks + 2,)),
            pltpu.SemaphoreType.DMA((blocks + 2,)),
        ],
        compiler_params=pltpu.CompilerParams(vmem_limit_bytes=VMEM_BYTES),
    )(owners, update, left_new, right_new)
    return (
        update.reshape(blocks, width, width),
        left_new.reshape(left_stats.shape),
        right_new.reshape(right_stats.shape),
    )


def solution(mesh):
    side = int(round(mesh.shape["dp"] ** 0.5))
    return jax.shard_map(
        functools.partial(local, side),
        mesh=mesh,
        in_specs=(
            P("dp", "shard", None, None),
            P("shard", None),
            P("dp", "shard", None, None, None),
            P("dp", "shard", None, None, None),
        ),
        out_specs=(
            P("shard", None, None),
            P("dp", "shard", None, None, None),
            P("dp", "shard", None, None, None),
        ),
        check_vma=False,
    )
```

```python
import functools

import jax
import jax.numpy as jnp
from jax import lax
from jax.experimental import pallas as pl
from jax.experimental.pallas import tpu as pltpu
from jax.sharding import PartitionSpec as P

ITERS = 4
DECAY = 0.9
RIDGE = 0.01
ROWS = 16
VMEM_BYTES = 56 * 1024 * 1024
BF16, F32 = jnp.bfloat16, jnp.float32
MESH = pl.DeviceIdType.MESH
A, B0, B1, C0, C1, D0, D1 = range(7)


def split(value):
    high = value.astype(BF16)
    return high, (value - high.astype(F32)).astype(BF16)


def product(first, second):
    (ah, al), (bh, bl) = first, second
    return jnp.dot(
        jnp.concatenate([ah, ah, al], axis=1),
        jnp.concatenate([bh, bl, bh], axis=0),
        preferred_element_type=F32,
    )


def total(value):
    return jnp.sum(jnp.sum(value, axis=0, keepdims=True), axis=1, keepdims=True)


def ranks_of(owners):
    ranks = []
    for b, owner in enumerate(owners):
        rank = jnp.int32(0)
        for other in owners[:b]:
            rank = rank + jnp.where(other == owner, 1, 0)
        ranks.append(rank)
    firsts = sum(jnp.where(rank == 0, 1, 0) for rank in ranks)
    places, first, second = [], jnp.int32(0), firsts
    for rank in ranks:
        places.append(jnp.where(rank == 0, first, second))
        first = first + jnp.where(rank == 0, 1, 0)
        second = second + jnp.where(rank == 0, 0, 1)
    return ranks, places


def chosen(tests, values):
    return sum(jnp.where(test, value, 0) for test, value in zip(tests, values))


class Root:
    def __init__(self, statistic, eye):
        width = statistic.shape[0]
        shift = total(jnp.where(eye, statistic, 0.0)) * (RIDGE / width)
        shifted = statistic + jnp.where(eye, shift, 0.0)
        scale = 2.5 / jnp.sqrt(total(shifted * shifted) + 1e-06)
        self.eye = eye
        self.gain = jnp.sqrt(jnp.sqrt(scale))
        self.power = scale * shifted
        self.next_factor()

    def next_factor(self):
        self.factor = split(jnp.where(self.eye, 1.25, 0.0) - 0.25 * self.power)

    def advance(self):
        square = split(product(self.factor, self.factor))
        fourth = split(product(square, square))
        self.power = product(fourth, split(self.power))
        self.next_factor()


def peers(side):
    me = lax.axis_index("dp")
    row, col = me // side, me % side

    def peer(k):
        return ((row + k // side) % side) * side + (col + k % side) % side

    return me, peer


def greet(n, peer):
    barrier = pltpu.get_barrier_semaphore()

    @pl.loop(1, n)
    def _(k):
        pl.semaphore_signal(barrier, inc=1, device_id={"dp": peer(k)}, device_id_type=MESH)

    pl.semaphore_wait(barrier, n - 1)


def sum_kernel(side, own_ref, g_ref, grad, parts, acc, picked, block_at, send, recv, local):
    n = side * side
    blocks = own_ref.shape[0]
    me, peer = peers(side)
    greet(n, peer)

    def copy(stage, k, src, dst):
        return pltpu.make_async_remote_copy(
            src_ref=src, dst_ref=dst, send_sem=send.at[stage, k], recv_sem=recv.at[stage, k],
            device_id={"dp": peer(k)}, device_id_type=MESH,
        )

    def part_copy(k):
        return copy(0, k, g_ref.at[:, peer(k)], parts.at[k])

    def slot_copy(k):
        return copy(1, k, picked.at[k], grad.at[:, me])

    @pl.loop(1, n)
    def _(k):
        part_copy(k).start()

    mine = pltpu.make_async_copy(g_ref.at[:, me], parts.at[0], local.at[0])
    mine.start()
    owners = [own_ref[b] for b in range(blocks)]
    ranks, _ = ranks_of(owners)

    @pl.loop(0, n)
    def _(k):
        to = peer(k)
        for slot in range(2):
            tests = [(o == to) & (r == slot) for o, r in zip(owners, ranks)]
            block_at[slot, k] = chosen(tests, range(blocks))

    mine.wait()
    acc[...] = parts[0].astype(F32)

    @pl.loop(1, n)
    def _(k):
        part_copy(k).wait_recv()
        acc[...] += parts[k].astype(F32)

    @pl.loop(1, n)
    def _(k):
        for slot in range(2):
            picked[k, slot] = acc[block_at[slot, k]]
        slot_copy(k).start()

    for slot in range(2):
        picked[0, slot] = acc[block_at[slot, 0]]
    own = pltpu.make_async_copy(picked.at[0], grad.at[:, me], local.at[1])
    own.start()

    @pl.loop(1, n)
    def _(k):
        part_copy(k).wait_send()

    own.wait()

    @pl.loop(1, n)
    def _(k):
        slot_copy(k).wait()


def root_kernel(own_ref, grad_ref, left, right, ready, left_out, right_out):
    blocks = own_ref.shape[0]
    width = left.shape[1]
    me = lax.axis_index("dp")
    owners = [own_ref[b] for b in range(blocks)]
    ranks, _ = ranks_of(owners)
    eye = lax.broadcasted_iota(jnp.int32, (width, width), 0) == lax.broadcasted_iota(
        jnp.int32, (width, width), 1
    )
    slots = []
    for slot in range(2):
        used = chosen([(o == me) & (r == slot) for o, r in zip(owners, ranks)], [1] * blocks) > 0
        value = jnp.where(used, grad_ref[slot].reshape(width, width), 0.0)
        plain, turned = split(value), split(value.T)
        left_new = DECAY * left[slot] + (1.0 - DECAY) * product(plain, turned)
        right_new = DECAY * right[slot] + (1.0 - DECAY) * product(turned, plain)
        left_out[slot] = left_new
        right_out[slot] = right_new
        slots.append((value, plain, Root(left_new, eye), Root(right_new, eye)))
    moved = [split(product(first.factor, plain)) for _, plain, first, _ in slots]
    moved = [product(m, s[3].factor) for m, s in zip(moved, slots)]
    for step in range(1, ITERS):
        roots = [root for s in slots for root in s[2:]]
        squares = [split(product(r.factor, r.factor)) for r in roots]
        fourths = [split(product(q, q)) for q in squares]
        for root, fourth in zip(roots, fourths):
            root.power = product(fourth, split(root.power))
            root.next_factor()
        moved = [split(product(s[2].factor, split(m))) for m, s in zip(moved, slots)]
        moved = [product(m, s[3].factor) for m, s in zip(moved, slots)]
    for slot, (value, _, first, second) in enumerate(slots):
        direction = (first.gain * second.gain) * moved[slot]
        count = 1.0 / (width * width)
        ratio = jnp.sqrt(total(value * value) * count) / jnp.sqrt(
            total(direction * direction) * count + 1e-06
        )
        ready[:, slot] = (direction * ratio).astype(BF16).reshape(-1, ROWS, width)


def spread_kernel(side, own_ref, ready, upd_ref, home, gather, owner_at, slot_at, send, recv, local):
    n = side * side
    blocks = own_ref.shape[0]
    me, peer = peers(side)
    greet(n, peer)

    def copy(stage, k, src, dst):
        return pltpu.make_async_remote_copy(
            src_ref=src, dst_ref=dst, send_sem=send.at[stage, k], recv_sem=recv.at[stage, k],
            device_id={"dp": peer(k)}, device_id_type=MESH,
        )

    def home_copy(k):
        return copy(0, k, ready.at[peer(k)], home.at[me])

    def gather_copy(k):
        return copy(1, k, gather, upd_ref.at[:, me])

    @pl.loop(1, n)
    def _(k):
        home_copy(k).start()

    mine = pltpu.make_async_copy(ready.at[me], home.at[me], local.at[0])
    mine.start()
    owners = [own_ref[b] for b in range(blocks)]
    ranks, _ = ranks_of(owners)
    for b in range(blocks):
        owner_at[b] = owners[b]
        slot_at[b] = jnp.where(ranks[b] == 0, 0, 1)
    mine.wait()

    @pl.loop(1, n)
    def _(k):
        home_copy(k).wait_recv()

    for b in range(blocks):
        gather[b] = home[owner_at[b], slot_at[b]]

    @pl.loop(1, n)
    def _(k):
        gather_copy(k).start()

    own = pltpu.make_async_copy(gather, upd_ref.at[:, me], local.at[1])
    own.start()

    @pl.loop(1, n)
    def _(k):
        home_copy(k).wait_send()

    own.wait()

    @pl.loop(1, n)
    def _(k):
        gather_copy(k).wait()


def local(side, grad_parts, owner_list, left_stats, right_stats):
    n = side * side
    _, blocks, width, _ = grad_parts.shape
    owners = owner_list[:, 0]
    tiles = (blocks, n, ROWS, width)
    pair = (2, width, width)
    vmem = pltpu.VMEM
    anywhere = pl.BlockSpec(memory_space=pl.ANY)
    scalars = pl.BlockSpec(memory_space=pltpu.SMEM)
    piece = (n, ROWS, width)
    dma = pltpu.SemaphoreType.DMA
    grad = pl.pallas_call(
        functools.partial(sum_kernel, side),
        out_shape=jax.ShapeDtypeStruct((2,) + piece, F32),
        in_specs=[scalars, anywhere],
        out_specs=anywhere,
        scratch_shapes=[
            vmem((n, blocks, ROWS, width), BF16),
            vmem((blocks, ROWS, width), F32),
            vmem((n, 2, ROWS, width), F32),
            pltpu.SMEM((2, n), jnp.int32),
            dma((2, n)),
            dma((2, n)),
            dma((2,)),
        ],
        compiler_params=pltpu.CompilerParams(
            collective_id=0, has_side_effects=True, vmem_limit_bytes=VMEM_BYTES
        ),
    )(owners, grad_parts.reshape(tiles))
    ready, left_new, right_new = pl.pallas_call(
        root_kernel,
        out_shape=(
            jax.ShapeDtypeStruct((n, 2, ROWS, width), BF16),
            jax.ShapeDtypeStruct(pair, F32),
            jax.ShapeDtypeStruct(pair, F32),
        ),
        in_specs=[scalars] + [pl.BlockSpec(memory_space=vmem)] * 3,
        out_specs=(pl.BlockSpec(memory_space=vmem),) * 3,
        compiler_params=pltpu.CompilerParams(vmem_limit_bytes=VMEM_BYTES),
    )(owners, grad, left_stats.reshape(pair), right_stats.reshape(pair))
    update = pl.pallas_call(
        functools.partial(spread_kernel, side),
        out_shape=jax.ShapeDtypeStruct(tiles, BF16),
        in_specs=[scalars, anywhere],
        out_specs=anywhere,
        scratch_shapes=[
            vmem((n, 2, ROWS, width), BF16),
            vmem((blocks, ROWS, width), BF16),
            pltpu.SMEM((blocks,), jnp.int32),
            pltpu.SMEM((blocks,), jnp.int32),
            dma((2, n)),
            dma((2, n)),
            dma((2,)),
        ],
        compiler_params=pltpu.CompilerParams(
            collective_id=1, has_side_effects=True, vmem_limit_bytes=VMEM_BYTES
        ),
    )(owners, ready)
    return (
        update.reshape(blocks, width, width),
        left_new.reshape(left_stats.shape),
        right_new.reshape(right_stats.shape),
    )


def solution(mesh):
    side = int(round(mesh.shape["dp"] ** 0.5))
    return jax.shard_map(
        functools.partial(local, side),
        mesh=mesh,
        in_specs=(
            P("dp", "shard", None, None),
            P("shard", None),
            P("dp", "shard", None, None, None),
            P("dp", "shard", None, None, None),
        ),
        out_specs=(
            P("shard", None, None),
            P("dp", "shard", None, None, None),
            P("dp", "shard", None, None, None),
        ),
        check_vma=False,
    )
```

```python
import functools

import jax
import jax.numpy as jnp
from jax import lax
from jax.experimental import pallas as pl
from jax.experimental.pallas import tpu as pltpu
from jax.sharding import PartitionSpec as P

ITERS = 4
DECAY = 0.9
RIDGE = 0.01
ROWS = 16
VMEM_BYTES = 56 * 1024 * 1024
HALF = 6
BF16, F32 = jnp.bfloat16, jnp.float32
MESH = pl.DeviceIdType.MESH


def split(value):
    high = value.astype(BF16)
    return high, (value - high.astype(F32)).astype(BF16)


def product(first, second):
    (ah, al), (bh, bl) = first, second
    return jnp.dot(
        jnp.concatenate([ah, ah, al], axis=1),
        jnp.concatenate([bh, bl, bh], axis=0),
        preferred_element_type=F32,
    )


def total(value):
    return jnp.sum(jnp.sum(value, axis=0, keepdims=True), axis=1, keepdims=True)


def ranks_of(owners):
    ranks, places, kinds = [], [], []
    for b, owner in enumerate(owners):
        rank = sum((jnp.where(other == owner, 1, 0) for other in owners[:b]), jnp.int32(0))
        later = sum((jnp.where(other == owner, 1, 0) for other in owners[b + 1 :]), jnp.int32(0))
        ranks.append(rank)
        kinds.append(jnp.where(rank > 0, 2, jnp.where(later > 0, 0, 1)))
    counts = [sum(jnp.where(kind == i, 1, 0) for kind in kinds) for i in range(2)]
    nexts = [jnp.int32(0), counts[0], counts[0] + counts[1]]
    for kind in kinds:
        places.append(jnp.where(kind == 0, nexts[0], jnp.where(kind == 1, nexts[1], nexts[2])))
        nexts = [at + jnp.where(kind == i, 1, 0) for i, at in enumerate(nexts)]
    return ranks, places


def chosen(tests, values):
    return sum(jnp.where(test, value, 0) for test, value in zip(tests, values))


class Root:
    def __init__(self, statistic, eye):
        width = statistic.shape[0]
        shift = total(jnp.where(eye, statistic, 0.0)) * (RIDGE / width)
        shifted = statistic + jnp.where(eye, shift, 0.0)
        scale = 2.5 / jnp.sqrt(total(shifted * shifted) + 1e-06)
        self.eye = eye
        self.gain = jnp.sqrt(jnp.sqrt(scale))
        self.power = scale * shifted
        self.next_factor()

    def next_factor(self):
        self.factor = split(jnp.where(self.eye, 1.25, 0.0) - 0.25 * self.power)

    def advance(self):
        square = split(product(self.factor, self.factor))
        fourth = split(product(square, square))
        self.power = product(fourth, split(self.power))
        self.next_factor()


def kernel(
    side, own_ref, g_ref, ls_ref, rs_ref, upd_ref, ln_ref, rn_ref,
    given, staged, parts0, parts1, acc0, acc1, picked0, picked1, grad0, grad1,
    left, right, left_out, right_out, ready0, ready1, home0, home1, lines0, lines1,
    block_at, owner_at, index_at,
    send, recv, send_line, recv_line, local,
):
    n = side * side
    blocks = own_ref.shape[0]
    width = left.shape[1]
    me = lax.axis_index("dp")
    row, col = me // side, me % side
    chunk = HALF // 2
    parts, acc, picked, grad = (parts0, parts1), (acc0, acc1), (picked0, picked1), (grad0, grad1)
    ready, home, lines = (ready0, ready1), (home0, home1), (lines0, lines1)

    def peer(k):
        return ((row + k // side) % side) * side + (col + k % side) % side

    def along(axis, k):
        if axis == 0:
            return row * side + (col + k) % side
        return ((row + k) % side) * side + col

    loads = [
        pltpu.make_async_copy(g_ref, given, local.at[0]),
        pltpu.make_async_copy(ls_ref, left, local.at[1]),
        pltpu.make_async_copy(rs_ref, right, local.at[2]),
    ]
    for load in loads:
        load.start()
    barrier = pltpu.get_barrier_semaphore()

    @pl.loop(1, n)
    def _(k):
        pl.semaphore_signal(barrier, inc=1, device_id={"dp": peer(k)}, device_id_type=MESH)

    owners = [own_ref[b] for b in range(blocks)]
    ranks, places = ranks_of(owners)

    @pl.loop(0, blocks)
    def _(p):
        tests = [at == p for at in places]
        block_at[p] = chosen(tests, range(blocks))
        owner_at[p] = chosen(tests, owners)

    def remote(src, dst, sent, landed, to):
        return pltpu.make_async_remote_copy(
            src_ref=src, dst_ref=dst, send_sem=sent, recv_sem=landed,
            device_id={"dp": to}, device_id_type=MESH,
        )

    def direct(what, half, k, src, dst):
        at = (2 * what + half, k)
        return remote(src, dst, send.at[at], recv.at[at], peer(k))

    def part_copy(half, k):
        return direct(
            0, half, k, staged.at[pl.ds(half * HALF, HALF), peer(k)], parts[half].at[k]
        )

    def slot_copy(half, k):
        return direct(1, half, k, picked[half].at[k], grad[half].at[me])

    def home_copy(half, k):
        return direct(2, half, k, ready[half].at[peer(k)], home[half].at[me])

    def line_copy(half, step, axis, k):
        at = (half, step, axis, k)
        held = lines[half].at[axis]
        if step == 0:
            src = dst = held.at[:, (col, row)[axis]]
            to = along(axis, k)
        else:
            src, dst, to = held, line_place(half, axis), along(1 - axis, k)
        return remote(src, dst, send_line.at[at], recv_line.at[at], to)

    def line_place(half, axis):
        ref = upd_ref.at[pl.ds(half * HALF + axis * chunk, chunk)]
        return ref.at[:, row] if axis == 0 else ref.at[:, :, col]

    loads[0].wait()
    for half in range(2):
        for p in range(half * HALF, (half + 1) * HALF):
            staged[p] = given[block_at[p]]
        if half == 0:
            pl.semaphore_wait(barrier, n - 1)

        @pl.loop(1, n)
        def _(k):
            part_copy(half, k).start()

    @pl.loop(0, n)
    def _(k):
        to = peer(k)
        for half in range(2):
            index = jnp.int32(0)
            for i in range(1, HALF):
                index = jnp.where(owner_at[half * HALF + i] == to, i, index)
            index_at[half, k] = index

    def mine(half, slot):
        tests = []
        for owner, rank, at in zip(owners, ranks, places):
            inside = (at < HALF) if half == 0 else (at >= HALF)
            tests.append((owner == me) & inside & ((rank == 0) if slot == 0 else (rank > 0)))
        return chosen(tests, [1] * blocks) > 0

    def to_owners(half):
        acc[half][...] = staged[pl.ds(half * HALF, HALF), me].astype(F32)

        @pl.loop(1, n)
        def _(k):
            part_copy(half, k).wait_recv()
            acc[half][...] += parts[half][k].astype(F32)

        @pl.loop(1, n)
        def _(k):
            picked[half][k] = acc[half][index_at[half, k]]
            slot_copy(half, k).start()

        grad[half][me] = acc[half][index_at[half, 0]]

    eye = lax.broadcasted_iota(jnp.int32, (width, width), 0) == lax.broadcasted_iota(
        jnp.int32, (width, width), 1
    )

    def solve(half, used, left_old, right_old, beside):
        @pl.loop(1, n)
        def _(k):
            slot_copy(half, k).wait_recv()

        value = jnp.where(used, grad[half][...].reshape(width, width), 0.0)
        plain, turned = split(value), split(value.T)
        left_new = DECAY * left_old + (1.0 - DECAY) * product(plain, turned)
        right_new = DECAY * right_old + (1.0 - DECAY) * product(turned, plain)
        if half == 0:
            left_out[0] = left_new
            right_out[0] = right_new
        else:
            for slot in range(2):
                here = mine(1, slot)
                for out, old, new in (
                    (left_out, left, left_new), (right_out, right, right_new)
                ):
                    rest = out[0] if slot == 0 else DECAY * old[1]
                    out[slot] = jnp.where(here, new, rest)
        first, second = Root(left_new, eye), Root(right_new, eye)
        moved = product(split(product(first.factor, plain)), second.factor)
        for step in range(1, ITERS):
            first.advance()
            second.advance()
            beside(step)
            moved = product(split(product(first.factor, split(moved))), second.factor)
        direction = (first.gain * second.gain) * moved
        count = 1.0 / (width * width)
        ratio = jnp.sqrt(total(value * value) * count) / jnp.sqrt(
            total(direction * direction) * count + 1e-06
        )
        ready[half][...] = (direction * ratio).astype(BF16).reshape(ready[half].shape)

        @pl.loop(1, n)
        def _(k):
            home_copy(half, k).start()

        home[half][me] = ready[half][me]

    def along_first(half):
        @pl.loop(1, n)
        def _(k):
            home_copy(half, k).wait_recv()

        for axis in range(2):
            for p in range(chunk):
                value = home[half][owner_at[half * HALF + axis * chunk + p]]
                lines[half][axis, p, (col, row)[axis]] = value
            for k in range(1, side):
                line_copy(half, 0, axis, k).start()

    rests = []

    def along_second(half):
        for axis in range(2):
            for k in range(1, side):
                line_copy(half, 0, axis, k).wait_recv()
            for k in range(1, side):
                line_copy(half, 1, axis, k).start()
            rest = pltpu.make_async_copy(
                lines[half].at[axis], line_place(half, axis), local.at[5 + 2 * half + axis]
            )
            rest.start()
            rests.append(rest)

    to_owners(0)
    loads[1].wait()
    loads[2].wait()

    def beside_first(step):
        if step == 2:
            to_owners(1)

    def beside_second(step):
        if step == 3:
            along_first(0)

    solve(0, mine(0, 0), left[0], right[0], beside_first)
    slot = jnp.where(mine(1, 1), 1, 0)
    used = mine(1, 0) | mine(1, 1)
    solve(1, used, left[slot], right[slot], beside_second)
    along_second(0)
    for ref, out, at in ((left_out, ln_ref, 3), (right_out, rn_ref, 4)):
        rest = pltpu.make_async_copy(ref, out, local.at[at])
        rest.start()
        rests.append(rest)
    along_first(1)
    along_second(1)

    @pl.loop(1, n)
    def _(k):
        for half in range(2):
            part_copy(half, k).wait_send()
            slot_copy(half, k).wait_send()
            home_copy(half, k).wait_send()

    for half in range(2):
        for axis in range(2):
            for k in range(1, side):
                line_copy(half, 0, axis, k).wait_send()
                line_copy(half, 1, axis, k).wait()
    for rest in rests:
        rest.wait()


def order_kernel(
    own_ref, upd_ref, ln_ref, rn_ref, out_ref, lo_ref, ro_ref, upd, left, right, into, out
):
    blocks = own_ref.shape[0]
    _, places = ranks_of([own_ref[b] for b in range(blocks)])
    moves = [
        (upd_ref.at[places[b]], upd.at[b], out_ref.at[b]) for b in range(blocks)
    ] + [(ln_ref, left, lo_ref), (rn_ref, right, ro_ref)]
    reads = [pltpu.make_async_copy(m[0], m[1], into.at[i]) for i, m in enumerate(moves)]
    writes = [pltpu.make_async_copy(m[1], m[2], out.at[i]) for i, m in enumerate(moves)]
    for read in reads:
        read.start()
    for read, write in zip(reads, writes):
        read.wait()
        write.start()
    for write in writes:
        write.wait()


def local(side, grad_parts, owner_list, left_stats, right_stats):
    n = side * side
    _, blocks, width, _ = grad_parts.shape
    owners = owner_list[:, 0]
    tiles = (blocks, n, ROWS, width)
    pair = (2, width, width)
    vmem = pltpu.VMEM
    anywhere = pl.BlockSpec(memory_space=pl.ANY)
    scalars = pl.BlockSpec(memory_space=pltpu.SMEM)
    piece = (n, ROWS, width)
    shapes = (
        jax.ShapeDtypeStruct((blocks, side, side, ROWS, width), BF16),
        jax.ShapeDtypeStruct(pair, F32),
        jax.ShapeDtypeStruct(pair, F32),
    )
    some = (HALF, ROWS, width)
    dma = pltpu.SemaphoreType.DMA
    update, left_new, right_new = pl.pallas_call(
        functools.partial(kernel, side),
        out_shape=shapes,
        in_specs=[scalars] + [anywhere] * 3,
        out_specs=(anywhere,) * 3,
        scratch_shapes=[vmem(tiles, BF16)] * 2
        + [vmem((n,) + some, BF16)] * 2
        + [vmem(some, F32)] * 2
        + [vmem(piece, F32)] * 4
        + [vmem(pair, F32)] * 4
        + [vmem(piece, BF16)] * 4
        + [vmem((2, HALF // 2, side, ROWS, width), BF16)] * 2
        + [
            pltpu.SMEM((blocks,), jnp.int32),
            pltpu.SMEM((blocks,), jnp.int32),
            pltpu.SMEM((2, n), jnp.int32),
            dma((6, n)),
            dma((6, n)),
            dma((2, 2, 2, side)),
            dma((2, 2, 2, side)),
            dma((9,)),
        ],
        compiler_params=pltpu.CompilerParams(
            collective_id=0, has_side_effects=True, vmem_limit_bytes=VMEM_BYTES
        ),
    )(
        owners,
        grad_parts.reshape(tiles),
        left_stats.reshape(pair),
        right_stats.reshape(pair),
    )
    update, left_new, right_new = pl.pallas_call(
        order_kernel,
        out_shape=shapes,
        in_specs=[scalars] + [anywhere] * 3,
        out_specs=(anywhere,) * 3,
        scratch_shapes=[
            vmem((blocks, side, side, ROWS, width), BF16),
            vmem(pair, F32),
            vmem(pair, F32),
            pltpu.SemaphoreType.DMA((blocks + 2,)),
            pltpu.SemaphoreType.DMA((blocks + 2,)),
        ],
        compiler_params=pltpu.CompilerParams(vmem_limit_bytes=VMEM_BYTES),
    )(owners, update, left_new, right_new)
    return (
        update.reshape(blocks, width, width),
        left_new.reshape(left_stats.shape),
        right_new.reshape(right_stats.shape),
    )


def solution(mesh):
    side = int(round(mesh.shape["dp"] ** 0.5))
    return jax.shard_map(
        functools.partial(local, side),
        mesh=mesh,
        in_specs=(
            P("dp", "shard", None, None),
            P("shard", None),
            P("dp", "shard", None, None, None),
            P("dp", "shard", None, None, None),
        ),
        out_specs=(
            P("shard", None, None),
            P("dp", "shard", None, None, None),
            P("dp", "shard", None, None, None),
        ),
        check_vma=False,
    )
```

```python
import functools

import jax
import jax.numpy as jnp
from jax import lax
from jax.experimental import pallas as pl
from jax.experimental.pallas import tpu as pltpu
from jax.sharding import PartitionSpec as P

ITERS = 4
DECAY = 0.9
RIDGE = 0.01
ROWS = 16
VMEM_BYTES = 56 * 1024 * 1024
HALF = 6
BF16, F32 = jnp.bfloat16, jnp.float32
MESH = pl.DeviceIdType.MESH


def split(value):
    high = value.astype(BF16)
    return high, (value - high.astype(F32)).astype(BF16)


def product(first, second):
    (ah, al), (bh, bl) = first, second
    return jnp.dot(
        jnp.concatenate([ah, ah, al], axis=1),
        jnp.concatenate([bh, bl, bh], axis=0),
        preferred_element_type=F32,
    )


def total(value):
    return jnp.sum(jnp.sum(value, axis=0, keepdims=True), axis=1, keepdims=True)


def ranks_of(owners):
    ranks, places, kinds = [], [], []
    for b, owner in enumerate(owners):
        rank = sum((jnp.where(other == owner, 1, 0) for other in owners[:b]), jnp.int32(0))
        later = sum((jnp.where(other == owner, 1, 0) for other in owners[b + 1 :]), jnp.int32(0))
        ranks.append(rank)
        kinds.append(jnp.where(rank > 0, 2, jnp.where(later > 0, 0, 1)))
    counts = [sum(jnp.where(kind == i, 1, 0) for kind in kinds) for i in range(2)]
    nexts = [jnp.int32(0), counts[0], counts[0] + counts[1]]
    for kind in kinds:
        places.append(jnp.where(kind == 0, nexts[0], jnp.where(kind == 1, nexts[1], nexts[2])))
        nexts = [at + jnp.where(kind == i, 1, 0) for i, at in enumerate(nexts)]
    return ranks, places


def chosen(tests, values):
    return sum(jnp.where(test, value, 0) for test, value in zip(tests, values))


class Root:
    def __init__(self, statistic, eye):
        width = statistic.shape[0]
        shift = total(jnp.where(eye, statistic, 0.0)) * (RIDGE / width)
        shifted = statistic + jnp.where(eye, shift, 0.0)
        scale = 2.5 / jnp.sqrt(total(shifted * shifted) + 1e-06)
        self.eye = eye
        self.gain = jnp.sqrt(jnp.sqrt(scale))
        self.power = scale * shifted
        self.next_factor()

    def next_factor(self):
        self.factor = split(jnp.where(self.eye, 1.25, 0.0) - 0.25 * self.power)

    def advance(self):
        square = split(product(self.factor, self.factor))
        fourth = split(product(square, square))
        self.power = product(fourth, split(self.power))
        self.next_factor()


DETOURS = (
    ((1, 2), (1, -1), (0, -1)),
    ((3, 2), (-1, -1), (0, -1)),
    ((2, 1), (-1, 1), (-1, 0)),
    ((2, 3), (-1, -1), (-1, 0)),
)


def kernel(
    side, own_ref, g_ref, ls_ref, rs_ref, upd_ref, ln_ref, rn_ref,
    given, staged, parts0, parts1, acc0, acc1, picked0, picked1, grad0, grad1,
    left, right, left_out, right_out, ready0, ready1, home0, home1, lines0, lines1,
    hop0, hop1, block_at, owner_at, index_at,
    send_hop, recv_hop, send, recv, send_line, recv_line, local,
):
    n = side * side
    blocks = own_ref.shape[0]
    width = left.shape[1]
    me = lax.axis_index("dp")
    row, col = me // side, me % side
    chunk = HALF // 2
    parts, acc, picked, grad = (parts0, parts1), (acc0, acc1), (picked0, picked1), (grad0, grad1)
    ready, home, lines = (ready0, ready1), (home0, home1), (lines0, lines1)
    hops = (hop0, hop1)

    def peer(k):
        return ((row + k // side) % side) * side + (col + k % side) % side

    def along(axis, k):
        if axis == 0:
            return row * side + (col + k) % side
        return ((row + k) % side) * side + col

    loads = [
        pltpu.make_async_copy(g_ref, given, local.at[0]),
        pltpu.make_async_copy(ls_ref, left, local.at[1]),
        pltpu.make_async_copy(rs_ref, right, local.at[2]),
    ]
    for load in loads:
        load.start()
    barrier = pltpu.get_barrier_semaphore()

    @pl.loop(1, n)
    def _(k):
        pl.semaphore_signal(barrier, inc=1, device_id={"dp": peer(k)}, device_id_type=MESH)

    owners = [own_ref[b] for b in range(blocks)]
    ranks, places = ranks_of(owners)

    @pl.loop(0, blocks)
    def _(p):
        tests = [at == p for at in places]
        block_at[p] = chosen(tests, range(blocks))
        owner_at[p] = chosen(tests, owners)

    def remote(src, dst, sent, landed, to):
        return pltpu.make_async_remote_copy(
            src_ref=src, dst_ref=dst, send_sem=sent, recv_sem=landed,
            device_id={"dp": to}, device_id_type=MESH,
        )

    def direct(what, half, k, src, dst):
        at = (2 * what + half, k)
        return remote(src, dst, send.at[at], recv.at[at], peer(k))

    def part_copy(half, k):
        return direct(
            0, half, k, staged.at[pl.ds(half * HALF, HALF), peer(k)], parts[half].at[k]
        )

    def at_steps(dy, dx):
        return ((row + dy + side) % side) * side + (col + dx + side) % side

    def hop_copy(half, i):
        (dy, dx), via, _ = DETOURS[i]
        src = staged.at[pl.ds(half * HALF, HALF), at_steps(dy, dx)]
        at = (half, 0, i)
        return remote(src, hops[half].at[i], send_hop.at[at], recv_hop.at[half, i], at_steps(*via))

    def last_copy(half, i):
        (dy, dx), _, last = DETOURS[i]
        k = dy * side + dx
        return remote(
            hops[half].at[i], parts[half].at[k], send_hop.at[half, 1, i], recv.at[half, k],
            at_steps(*last),
        )

    def send_on(half):
        for i in range(len(DETOURS)):
            hop_copy(half, i).wait_recv()
            last_copy(half, i).start()

    straight = [k for k in range(1, n) if (k // side, k % side) not in [d[0] for d in DETOURS]]

    def slot_copy(half, k):
        return direct(1, half, k, picked[half].at[k], grad[half].at[me])

    def home_copy(half, k):
        return direct(2, half, k, ready[half].at[peer(k)], home[half].at[me])

    def line_copy(half, step, axis, k):
        at = (half, step, axis, k)
        held = lines[half].at[axis]
        if step == 0:
            src = dst = held.at[:, (col, row)[axis]]
            to = along(axis, k)
        else:
            to = along(1 - axis, k)
            if k == 2:
                src, dst = held.at[pl.ds(0, 1)], line_place(half, axis, 0, 0, 1)
            else:
                src, dst = held, line_place(half, axis)
        return remote(src, dst, send_line.at[at], recv_line.at[at], to)

    def line_place(half, axis, step=0, first=0, size=chunk):
        ref = upd_ref.at[pl.ds(half * HALF + axis * chunk + first, size)]
        if axis == 0:
            return ref.at[:, (row + step) % side]
        return ref.at[:, :, (col + step) % side]

    def line_pass(half, axis):
        ref = line_place(half, axis, 1, 1, chunk - 1)
        at = (half, 1, axis, 0)
        return remote(ref, ref, send_line.at[at], recv_line.at[at], along(1 - axis, side - 1))

    def pass_lines(half):
        for axis in range(2):
            line_copy(half, 1, axis, side - 1).wait_recv()
            line_pass(half, axis).start()

    loads[0].wait()
    for half in range(2):
        for p in range(half * HALF, (half + 1) * HALF):
            staged[p] = given[block_at[p]]
        if half == 0:
            pl.semaphore_wait(barrier, n - 1)

        for i in range(len(DETOURS)):
            hop_copy(half, i).start()
        for k in straight:
            part_copy(half, k).start()

    @pl.loop(0, n)
    def _(k):
        to = peer(k)
        for half in range(2):
            index = jnp.int32(0)
            for i in range(1, HALF):
                index = jnp.where(owner_at[half * HALF + i] == to, i, index)
            index_at[half, k] = index

    def mine(half, slot):
        tests = []
        for owner, rank, at in zip(owners, ranks, places):
            inside = (at < HALF) if half == 0 else (at >= HALF)
            tests.append((owner == me) & inside & ((rank == 0) if slot == 0 else (rank > 0)))
        return chosen(tests, [1] * blocks) > 0

    def to_owners(half):
        acc[half][...] = staged[pl.ds(half * HALF, HALF), me].astype(F32)

        @pl.loop(1, n)
        def _(k):
            part_copy(half, k).wait_recv()
            acc[half][...] += parts[half][k].astype(F32)

        @pl.loop(1, n)
        def _(k):
            picked[half][k] = acc[half][index_at[half, k]]
            slot_copy(half, k).start()

        grad[half][me] = acc[half][index_at[half, 0]]

    eye = lax.broadcasted_iota(jnp.int32, (width, width), 0) == lax.broadcasted_iota(
        jnp.int32, (width, width), 1
    )

    def solve(half, used, left_old, right_old, beside):
        @pl.loop(1, n)
        def _(k):
            slot_copy(half, k).wait_recv()

        value = jnp.where(used, grad[half][...].reshape(width, width), 0.0)
        plain, turned = split(value), split(value.T)
        left_new = DECAY * left_old + (1.0 - DECAY) * product(plain, turned)
        right_new = DECAY * right_old + (1.0 - DECAY) * product(turned, plain)
        if half == 0:
            left_out[0] = left_new
            right_out[0] = right_new
        else:
            for slot in range(2):
                here = mine(1, slot)
                for out, old, new in (
                    (left_out, left, left_new), (right_out, right, right_new)
                ):
                    rest = out[0] if slot == 0 else DECAY * old[1]
                    out[slot] = jnp.where(here, new, rest)
        first, second = Root(left_new, eye), Root(right_new, eye)
        moved = product(split(product(first.factor, plain)), second.factor)
        for step in range(1, ITERS):
            first.advance()
            second.advance()
            beside(step)
            moved = product(split(product(first.factor, split(moved))), second.factor)
        direction = (first.gain * second.gain) * moved
        count = 1.0 / (width * width)
        ratio = jnp.sqrt(total(value * value) * count) / jnp.sqrt(
            total(direction * direction) * count + 1e-06
        )
        ready[half][...] = (direction * ratio).astype(BF16).reshape(ready[half].shape)

        @pl.loop(1, n)
        def _(k):
            home_copy(half, k).start()

        home[half][me] = ready[half][me]

    def along_first(half):
        @pl.loop(1, n)
        def _(k):
            home_copy(half, k).wait_recv()

        for axis in range(2):
            for p in range(chunk):
                value = home[half][owner_at[half * HALF + axis * chunk + p]]
                lines[half][axis, p, (col, row)[axis]] = value
            for k in range(1, side):
                line_copy(half, 0, axis, k).start()

    rests = []

    def along_second(half):
        for axis in range(2):
            for k in range(1, side):
                line_copy(half, 0, axis, k).wait_recv()
            for k in range(1, side):
                line_copy(half, 1, axis, k).start()
            rest = pltpu.make_async_copy(
                lines[half].at[axis], line_place(half, axis), local.at[5 + 2 * half + axis]
            )
            rest.start()
            rests.append(rest)

    send_on(0)
    to_owners(0)
    send_on(1)
    loads[1].wait()
    loads[2].wait()

    def beside_first(step):
        if step == 2:
            to_owners(1)

    def beside_second(step):
        if step == 3:
            along_first(0)

    solve(0, mine(0, 0), left[0], right[0], beside_first)
    slot = jnp.where(mine(1, 1), 1, 0)
    used = mine(1, 0) | mine(1, 1)
    solve(1, used, left[slot], right[slot], beside_second)
    along_second(0)
    for ref, out, at in ((left_out, ln_ref, 3), (right_out, rn_ref, 4)):
        rest = pltpu.make_async_copy(ref, out, local.at[at])
        rest.start()
        rests.append(rest)
    along_first(1)
    pass_lines(0)
    along_second(1)
    pass_lines(1)

    @pl.loop(1, n)
    def _(k):
        for half in range(2):
            slot_copy(half, k).wait_send()
            home_copy(half, k).wait_send()

    for half in range(2):
        for k in straight:
            part_copy(half, k).wait_send()
        for i in range(len(DETOURS)):
            hop_copy(half, i).wait_send()
            last_copy(half, i).wait_send()
        for axis in range(2):
            line_pass(half, axis).wait()
            for k in range(1, side):
                line_copy(half, 0, axis, k).wait_send()
                line_copy(half, 1, axis, k).wait_send()
                if k < side - 1:
                    line_copy(half, 1, axis, k).wait_recv()
    for rest in rests:
        rest.wait()


def order_kernel(
    own_ref, upd_ref, ln_ref, rn_ref, out_ref, lo_ref, ro_ref, upd, left, right, into, out
):
    blocks = own_ref.shape[0]
    _, places = ranks_of([own_ref[b] for b in range(blocks)])
    moves = [
        (upd_ref.at[places[b]], upd.at[b], out_ref.at[b]) for b in range(blocks)
    ] + [(ln_ref, left, lo_ref), (rn_ref, right, ro_ref)]
    reads = [pltpu.make_async_copy(m[0], m[1], into.at[i]) for i, m in enumerate(moves)]
    writes = [pltpu.make_async_copy(m[1], m[2], out.at[i]) for i, m in enumerate(moves)]
    for read in reads:
        read.start()
    for read, write in zip(reads, writes):
        read.wait()
        write.start()
    for write in writes:
        write.wait()


def local(side, grad_parts, owner_list, left_stats, right_stats):
    n = side * side
    _, blocks, width, _ = grad_parts.shape
    owners = owner_list[:, 0]
    tiles = (blocks, n, ROWS, width)
    pair = (2, width, width)
    vmem = pltpu.VMEM
    anywhere = pl.BlockSpec(memory_space=pl.ANY)
    scalars = pl.BlockSpec(memory_space=pltpu.SMEM)
    piece = (n, ROWS, width)
    shapes = (
        jax.ShapeDtypeStruct((blocks, side, side, ROWS, width), BF16),
        jax.ShapeDtypeStruct(pair, F32),
        jax.ShapeDtypeStruct(pair, F32),
    )
    some = (HALF, ROWS, width)
    dma = pltpu.SemaphoreType.DMA
    update, left_new, right_new = pl.pallas_call(
        functools.partial(kernel, side),
        out_shape=shapes,
        in_specs=[scalars] + [anywhere] * 3,
        out_specs=(anywhere,) * 3,
        scratch_shapes=[vmem(tiles, BF16)] * 2
        + [vmem((n,) + some, BF16)] * 2
        + [vmem(some, F32)] * 2
        + [vmem(piece, F32)] * 4
        + [vmem(pair, F32)] * 4
        + [vmem(piece, BF16)] * 4
        + [vmem((2, HALF // 2, side, ROWS, width), BF16)] * 2
        + [vmem((len(DETOURS),) + some, BF16)] * 2
        + [
            pltpu.SMEM((blocks,), jnp.int32),
            pltpu.SMEM((blocks,), jnp.int32),
            pltpu.SMEM((2, n), jnp.int32),
            dma((2, 2, len(DETOURS))),
            dma((2, len(DETOURS))),
            dma((6, n)),
            dma((6, n)),
            dma((2, 2, 2, side)),
            dma((2, 2, 2, side)),
            dma((9,)),
        ],
        compiler_params=pltpu.CompilerParams(
            collective_id=0, has_side_effects=True, vmem_limit_bytes=VMEM_BYTES
        ),
    )(
        owners,
        grad_parts.reshape(tiles),
        left_stats.reshape(pair),
        right_stats.reshape(pair),
    )
    update, left_new, right_new = pl.pallas_call(
        order_kernel,
        out_shape=shapes,
        in_specs=[scalars] + [anywhere] * 3,
        out_specs=(anywhere,) * 3,
        scratch_shapes=[
            vmem((blocks, side, side, ROWS, width), BF16),
            vmem(pair, F32),
            vmem(pair, F32),
            pltpu.SemaphoreType.DMA((blocks + 2,)),
            pltpu.SemaphoreType.DMA((blocks + 2,)),
        ],
        compiler_params=pltpu.CompilerParams(vmem_limit_bytes=VMEM_BYTES),
    )(owners, update, left_new, right_new)
    return (
        update.reshape(blocks, width, width),
        left_new.reshape(left_stats.shape),
        right_new.reshape(right_stats.shape),
    )


def solution(mesh):
    side = int(round(mesh.shape["dp"] ** 0.5))
    return jax.shard_map(
        functools.partial(local, side),
        mesh=mesh,
        in_specs=(
            P("dp", "shard", None, None),
            P("shard", None),
            P("dp", "shard", None, None, None),
            P("dp", "shard", None, None, None),
        ),
        out_specs=(
            P("shard", None, None),
            P("dp", "shard", None, None, None),
            P("dp", "shard", None, None, None),
        ),
        check_vma=False,
    )
```

```python
import functools

import jax
import jax.numpy as jnp
from jax import lax
from jax.experimental import pallas as pl
from jax.experimental.pallas import tpu as pltpu
from jax.sharding import PartitionSpec as P

ITERS = 4
DECAY = 0.9
RIDGE = 0.01
ROWS = 16
VMEM_BYTES = 56 * 1024 * 1024
HALF = 6
BF16, F32 = jnp.bfloat16, jnp.float32
MESH = pl.DeviceIdType.MESH


def split(value):
    high = value.astype(BF16)
    return high, (value - high.astype(F32)).astype(BF16)


def product(first, second):
    (ah, al), (bh, bl) = first, second
    return jnp.dot(
        jnp.concatenate([ah, ah, al], axis=1),
        jnp.concatenate([bh, bl, bh], axis=0),
        preferred_element_type=F32,
    )


def total(value):
    return jnp.sum(jnp.sum(value, axis=0, keepdims=True), axis=1, keepdims=True)


def ranks_of(owners):
    ranks, places, kinds = [], [], []
    for b, owner in enumerate(owners):
        rank = sum((jnp.where(other == owner, 1, 0) for other in owners[:b]), jnp.int32(0))
        later = sum((jnp.where(other == owner, 1, 0) for other in owners[b + 1 :]), jnp.int32(0))
        ranks.append(rank)
        kinds.append(jnp.where(rank > 0, 2, jnp.where(later > 0, 0, 1)))
    counts = [sum(jnp.where(kind == i, 1, 0) for kind in kinds) for i in range(2)]
    nexts = [jnp.int32(0), counts[0], counts[0] + counts[1]]
    for kind in kinds:
        places.append(jnp.where(kind == 0, nexts[0], jnp.where(kind == 1, nexts[1], nexts[2])))
        nexts = [at + jnp.where(kind == i, 1, 0) for i, at in enumerate(nexts)]
    return ranks, places


def chosen(tests, values):
    return sum(jnp.where(test, value, 0) for test, value in zip(tests, values))


class Root:
    def __init__(self, statistic, eye):
        width = statistic.shape[0]
        shift = total(jnp.where(eye, statistic, 0.0)) * (RIDGE / width)
        shifted = statistic + jnp.where(eye, shift, 0.0)
        scale = 2.5 / jnp.sqrt(total(shifted * shifted) + 1e-06)
        self.eye = eye
        self.gain = jnp.sqrt(jnp.sqrt(scale))
        self.power = scale * shifted
        self.next_factor()

    def next_factor(self):
        self.factor = split(jnp.where(self.eye, 1.25, 0.0) - 0.25 * self.power)

    def advance(self):
        square = split(product(self.factor, self.factor))
        fourth = split(product(square, square))
        self.power = product(fourth, split(self.power))
        self.next_factor()


def kernel(
    side, own_ref, g_ref, ls_ref, rs_ref, upd_ref, ln_ref, rn_ref,
    given, staged, parts0, parts1, acc0, acc1, picked0, picked1, grad0, grad1,
    left, right, left_out, right_out, ready0, ready1, home0, home1, lines0, lines1,
    block_at, owner_at, index_at,
    send, recv, send_line, recv_line, local,
):
    n = side * side
    blocks = own_ref.shape[0]
    width = left.shape[1]
    me = lax.axis_index("dp")
    row, col = me // side, me % side
    chunk = HALF // 2
    parts, acc, picked, grad = (parts0, parts1), (acc0, acc1), (picked0, picked1), (grad0, grad1)
    ready, home, lines = (ready0, ready1), (home0, home1), (lines0, lines1)

    def peer(k):
        return ((row + k // side) % side) * side + (col + k % side) % side

    def along(axis, k):
        if axis == 0:
            return row * side + (col + k) % side
        return ((row + k) % side) * side + col

    core = lax.axis_index("shard") % 2

    def turned_round(i):
        return 1 + (i + me + core * (n // 2 - 1)) % (n - 1)

    loads = [
        pltpu.make_async_copy(g_ref, given, local.at[0]),
        pltpu.make_async_copy(ls_ref, left, local.at[1]),
        pltpu.make_async_copy(rs_ref, right, local.at[2]),
    ]
    for load in loads:
        load.start()
    barrier = pltpu.get_barrier_semaphore()

    @pl.loop(1, n)
    def _(k):
        pl.semaphore_signal(barrier, inc=1, device_id={"dp": peer(k)}, device_id_type=MESH)

    owners = [own_ref[b] for b in range(blocks)]
    ranks, places = ranks_of(owners)

    @pl.loop(0, blocks)
    def _(p):
        tests = [at == p for at in places]
        block_at[p] = chosen(tests, range(blocks))
        owner_at[p] = chosen(tests, owners)

    def remote(src, dst, sent, landed, to):
        return pltpu.make_async_remote_copy(
            src_ref=src, dst_ref=dst, send_sem=sent, recv_sem=landed,
            device_id={"dp": to}, device_id_type=MESH,
        )

    def direct(what, half, k, src, dst):
        at = (2 * what + half, k)
        return remote(src, dst, send.at[at], recv.at[at], peer(k))

    def part_copy(half, k):
        return direct(
            0, half, k, staged.at[pl.ds(half * HALF, HALF), peer(k)], parts[half].at[k]
        )

    def slot_copy(half, k):
        return direct(1, half, k, picked[half].at[k], grad[half].at[me])

    def home_copy(half, k):
        return direct(2, half, k, ready[half].at[peer(k)], home[half].at[me])

    def line_copy(half, step, axis, k):
        at = (half, step, axis, k)
        held = lines[half].at[axis]
        if step == 0:
            src = dst = held.at[:, (col, row)[axis]]
            to = along(axis, k)
        else:
            src, dst, to = held, line_place(half, axis), along(1 - axis, k)
        return remote(src, dst, send_line.at[at], recv_line.at[at], to)

    def line_place(half, axis):
        ref = upd_ref.at[pl.ds(half * HALF + axis * chunk, chunk)]
        return ref.at[:, row] if axis == 0 else ref.at[:, :, col]

    loads[0].wait()
    for half in range(2):
        for p in range(half * HALF, (half + 1) * HALF):
            staged[p] = given[block_at[p]]
        if half == 0:
            pl.semaphore_wait(barrier, n - 1)

        @pl.loop(0, n - 1)
        def _(i):
            part_copy(half, turned_round(i)).start()

    @pl.loop(0, n)
    def _(k):
        to = peer(k)
        for half in range(2):
            index = jnp.int32(0)
            for i in range(1, HALF):
                index = jnp.where(owner_at[half * HALF + i] == to, i, index)
            index_at[half, k] = index

    def mine(half, slot):
        tests = []
        for owner, rank, at in zip(owners, ranks, places):
            inside = (at < HALF) if half == 0 else (at >= HALF)
            tests.append((owner == me) & inside & ((rank == 0) if slot == 0 else (rank > 0)))
        return chosen(tests, [1] * blocks) > 0

    def to_owners(half):
        acc[half][...] = staged[pl.ds(half * HALF, HALF), me].astype(F32)

        @pl.loop(1, n)
        def _(k):
            part_copy(half, k).wait_recv()
            acc[half][...] += parts[half][k].astype(F32)

        @pl.loop(0, n - 1)
        def _(i):
            k = turned_round(i)
            picked[half][k] = acc[half][index_at[half, k]]
            slot_copy(half, k).start()

        grad[half][me] = acc[half][index_at[half, 0]]

    eye = lax.broadcasted_iota(jnp.int32, (width, width), 0) == lax.broadcasted_iota(
        jnp.int32, (width, width), 1
    )

    def solve(half, used, left_old, right_old, beside):
        @pl.loop(1, n)
        def _(k):
            slot_copy(half, k).wait_recv()

        value = jnp.where(used, grad[half][...].reshape(width, width), 0.0)
        plain, turned = split(value), split(value.T)
        left_new = DECAY * left_old + (1.0 - DECAY) * product(plain, turned)
        right_new = DECAY * right_old + (1.0 - DECAY) * product(turned, plain)
        if half == 0:
            left_out[0] = left_new
            right_out[0] = right_new
        else:
            for slot in range(2):
                here = mine(1, slot)
                for out, old, new in (
                    (left_out, left, left_new), (right_out, right, right_new)
                ):
                    rest = out[0] if slot == 0 else DECAY * old[1]
                    out[slot] = jnp.where(here, new, rest)
        first, second = Root(left_new, eye), Root(right_new, eye)
        moved = product(split(product(first.factor, plain)), second.factor)
        for step in range(1, ITERS):
            first.advance()
            second.advance()
            beside(step)
            moved = product(split(product(first.factor, split(moved))), second.factor)
        direction = (first.gain * second.gain) * moved
        count = 1.0 / (width * width)
        ratio = jnp.sqrt(total(value * value) * count) / jnp.sqrt(
            total(direction * direction) * count + 1e-06
        )
        ready[half][...] = (direction * ratio).astype(BF16).reshape(ready[half].shape)

        @pl.loop(0, n - 1)
        def _(i):
            home_copy(half, turned_round(i)).start()

        home[half][me] = ready[half][me]

    def along_first(half):
        @pl.loop(1, n)
        def _(k):
            home_copy(half, k).wait_recv()

        for axis in range(2):
            for p in range(chunk):
                value = home[half][owner_at[half * HALF + axis * chunk + p]]
                lines[half][axis, p, (col, row)[axis]] = value
        for i in range(side - 1):
            for axis in range(2):
                line_copy(half, 0, axis, line_turn(axis, i)).start()

    rests = []

    def line_turn(axis, i):
        return 1 + (i + row + col + core + axis) % (side - 1)

    def along_second(half):
        for axis in range(2):
            for k in range(1, side):
                line_copy(half, 0, axis, k).wait_recv()
        for i in range(side - 1):
            for axis in range(2):
                line_copy(half, 1, axis, line_turn(axis, i)).start()
        for axis in range(2):
            rest = pltpu.make_async_copy(
                lines[half].at[axis], line_place(half, axis), local.at[5 + 2 * half + axis]
            )
            rest.start()
            rests.append(rest)

    to_owners(0)
    loads[1].wait()
    loads[2].wait()

    def beside_first(step):
        if step == 2:
            to_owners(1)

    def beside_second(step):
        if step == 3:
            along_first(0)

    solve(0, mine(0, 0), left[0], right[0], beside_first)
    slot = jnp.where(mine(1, 1), 1, 0)
    used = mine(1, 0) | mine(1, 1)
    solve(1, used, left[slot], right[slot], beside_second)
    along_second(0)
    for ref, out, at in ((left_out, ln_ref, 3), (right_out, rn_ref, 4)):
        rest = pltpu.make_async_copy(ref, out, local.at[at])
        rest.start()
        rests.append(rest)
    along_first(1)
    along_second(1)

    @pl.loop(1, n)
    def _(k):
        for half in range(2):
            part_copy(half, k).wait_send()
            slot_copy(half, k).wait_send()
            home_copy(half, k).wait_send()

    for half in range(2):
        for axis in range(2):
            for k in range(1, side):
                line_copy(half, 0, axis, k).wait_send()
                line_copy(half, 1, axis, k).wait()
    for rest in rests:
        rest.wait()


def order_kernel(
    own_ref, upd_ref, ln_ref, rn_ref, out_ref, lo_ref, ro_ref, upd, left, right, into, out
):
    blocks = own_ref.shape[0]
    _, places = ranks_of([own_ref[b] for b in range(blocks)])
    moves = [
        (upd_ref.at[places[b]], upd.at[b], out_ref.at[b]) for b in range(blocks)
    ] + [(ln_ref, left, lo_ref), (rn_ref, right, ro_ref)]
    reads = [pltpu.make_async_copy(m[0], m[1], into.at[i]) for i, m in enumerate(moves)]
    writes = [pltpu.make_async_copy(m[1], m[2], out.at[i]) for i, m in enumerate(moves)]
    for read in reads:
        read.start()
    for read, write in zip(reads, writes):
        read.wait()
        write.start()
    for write in writes:
        write.wait()


def local(side, grad_parts, owner_list, left_stats, right_stats):
    n = side * side
    _, blocks, width, _ = grad_parts.shape
    owners = owner_list[:, 0]
    tiles = (blocks, n, ROWS, width)
    pair = (2, width, width)
    vmem = pltpu.VMEM
    anywhere = pl.BlockSpec(memory_space=pl.ANY)
    scalars = pl.BlockSpec(memory_space=pltpu.SMEM)
    piece = (n, ROWS, width)
    shapes = (
        jax.ShapeDtypeStruct((blocks, side, side, ROWS, width), BF16),
        jax.ShapeDtypeStruct(pair, F32),
        jax.ShapeDtypeStruct(pair, F32),
    )
    some = (HALF, ROWS, width)
    dma = pltpu.SemaphoreType.DMA
    update, left_new, right_new = pl.pallas_call(
        functools.partial(kernel, side),
        out_shape=shapes,
        in_specs=[scalars] + [anywhere] * 3,
        out_specs=(anywhere,) * 3,
        scratch_shapes=[vmem(tiles, BF16)] * 2
        + [vmem((n,) + some, BF16)] * 2
        + [vmem(some, F32)] * 2
        + [vmem(piece, F32)] * 4
        + [vmem(pair, F32)] * 4
        + [vmem(piece, BF16)] * 4
        + [vmem((2, HALF // 2, side, ROWS, width), BF16)] * 2
        + [
            pltpu.SMEM((blocks,), jnp.int32),
            pltpu.SMEM((blocks,), jnp.int32),
            pltpu.SMEM((2, n), jnp.int32),
            dma((6, n)),
            dma((6, n)),
            dma((2, 2, 2, side)),
            dma((2, 2, 2, side)),
            dma((9,)),
        ],
        compiler_params=pltpu.CompilerParams(
            collective_id=0, has_side_effects=True, vmem_limit_bytes=VMEM_BYTES
        ),
    )(
        owners,
        grad_parts.reshape(tiles),
        left_stats.reshape(pair),
        right_stats.reshape(pair),
    )
    update, left_new, right_new = pl.pallas_call(
        order_kernel,
        out_shape=shapes,
        in_specs=[scalars] + [anywhere] * 3,
        out_specs=(anywhere,) * 3,
        scratch_shapes=[
            vmem((blocks, side, side, ROWS, width), BF16),
            vmem(pair, F32),
            vmem(pair, F32),
            pltpu.SemaphoreType.DMA((blocks + 2,)),
            pltpu.SemaphoreType.DMA((blocks + 2,)),
        ],
        compiler_params=pltpu.CompilerParams(vmem_limit_bytes=VMEM_BYTES),
    )(owners, update, left_new, right_new)
    return (
        update.reshape(blocks, width, width),
        left_new.reshape(left_stats.shape),
        right_new.reshape(right_stats.shape),
    )


def solution(mesh):
    side = int(round(mesh.shape["dp"] ** 0.5))
    return jax.shard_map(
        functools.partial(local, side),
        mesh=mesh,
        in_specs=(
            P("dp", "shard", None, None),
            P("shard", None),
            P("dp", "shard", None, None, None),
            P("dp", "shard", None, None, None),
        ),
        out_specs=(
            P("shard", None, None),
            P("dp", "shard", None, None, None),
            P("dp", "shard", None, None, None),
        ),
        check_vma=False,
    )
```

```python
import functools

import jax
import jax.numpy as jnp
from jax import lax
from jax.experimental import pallas as pl
from jax.experimental.pallas import tpu as pltpu
from jax.sharding import PartitionSpec as P

ITERS = 4
DECAY = 0.9
RIDGE = 0.01
ROWS = 16
VMEM_BYTES = 56 * 1024 * 1024
HALF = 6
BF16, F32 = jnp.bfloat16, jnp.float32
MESH = pl.DeviceIdType.MESH


def split(value):
    high = value.astype(BF16)
    return high, (value - high.astype(F32)).astype(BF16)


def product(first, second):
    (ah, al), (bh, bl) = first, second
    return jnp.dot(
        jnp.concatenate([ah, ah, al], axis=1),
        jnp.concatenate([bh, bl, bh], axis=0),
        preferred_element_type=F32,
    )


def total(value):
    return jnp.sum(jnp.sum(value, axis=0, keepdims=True), axis=1, keepdims=True)


def ranks_of(owners):
    ranks, places, kinds = [], [], []
    for b, owner in enumerate(owners):
        rank = sum((jnp.where(other == owner, 1, 0) for other in owners[:b]), jnp.int32(0))
        later = sum((jnp.where(other == owner, 1, 0) for other in owners[b + 1 :]), jnp.int32(0))
        ranks.append(rank)
        kinds.append(jnp.where(rank > 0, 2, jnp.where(later > 0, 0, 1)))
    counts = [sum(jnp.where(kind == i, 1, 0) for kind in kinds) for i in range(2)]
    nexts = [jnp.int32(0), counts[0], counts[0] + counts[1]]
    for kind in kinds:
        places.append(jnp.where(kind == 0, nexts[0], jnp.where(kind == 1, nexts[1], nexts[2])))
        nexts = [at + jnp.where(kind == i, 1, 0) for i, at in enumerate(nexts)]
    return ranks, places


def chosen(tests, values):
    return sum(jnp.where(test, value, 0) for test, value in zip(tests, values))


class Root:
    def __init__(self, statistic, eye):
        width = statistic.shape[0]
        shift = total(jnp.where(eye, statistic, 0.0)) * (RIDGE / width)
        shifted = statistic + jnp.where(eye, shift, 0.0)
        scale = 2.5 / jnp.sqrt(total(shifted * shifted) + 1e-06)
        self.eye = eye
        self.gain = jnp.sqrt(jnp.sqrt(scale))
        self.power = scale * shifted
        self.next_factor()

    def next_factor(self):
        self.factor = split(jnp.where(self.eye, 1.25, 0.0) - 0.25 * self.power)

    def advance(self):
        square = split(product(self.factor, self.factor))
        fourth = split(product(square, square))
        self.power = product(fourth, split(self.power))
        self.next_factor()


def kernel(
    side, own_ref, g_ref, ls_ref, rs_ref, upd_ref, ln_ref, rn_ref,
    given, staged, parts0, parts1, acc0, acc1, picked0, picked1, grad0, grad1,
    left, right, left_out, right_out, ready0, ready1, home0, home1, lines0, lines1,
    block_at, owner_at, index_at,
    send, recv, send_line, recv_line, local,
):
    n = side * side
    blocks = own_ref.shape[0]
    width = left.shape[1]
    me = lax.axis_index("dp")
    row, col = me // side, me % side
    chunk = HALF // 2
    parts, acc, picked, grad = (parts0, parts1), (acc0, acc1), (picked0, picked1), (grad0, grad1)
    ready, home, lines = (ready0, ready1), (home0, home1), (lines0, lines1)

    def peer(k):
        return ((row + k // side) % side) * side + (col + k % side) % side

    def along(axis, k):
        if axis == 0:
            return row * side + (col + k) % side
        return ((row + k) % side) * side + col

    core = lax.axis_index("shard") % 2

    def turned_round(i):
        return 1 + (i + me + core * (n // 2 - 1)) % (n - 1)

    loads = [
        pltpu.make_async_copy(g_ref, given, local.at[0]),
        pltpu.make_async_copy(ls_ref, left, local.at[1]),
        pltpu.make_async_copy(rs_ref, right, local.at[2]),
    ]
    for load in loads:
        load.start()
    barrier = pltpu.get_barrier_semaphore()

    @pl.loop(1, n)
    def _(k):
        pl.semaphore_signal(barrier, inc=1, device_id={"dp": peer(k)}, device_id_type=MESH)

    owners = [own_ref[b] for b in range(blocks)]
    ranks, places = ranks_of(owners)

    @pl.loop(0, blocks)
    def _(p):
        tests = [at == p for at in places]
        block_at[p] = chosen(tests, range(blocks))
        owner_at[p] = chosen(tests, owners)

    def remote(src, dst, sent, landed, to):
        return pltpu.make_async_remote_copy(
            src_ref=src, dst_ref=dst, send_sem=sent, recv_sem=landed,
            device_id={"dp": to}, device_id_type=MESH,
        )

    def direct(what, half, k, src, dst):
        at = (2 * what + half, k)
        return remote(src, dst, send.at[at], recv.at[at], peer(k))

    def part_copy(half, k):
        return direct(
            0, half, k, staged.at[half, peer(k)], parts[half].at[k]
        )

    def slot_copy(half, k):
        return direct(1, half, k, picked[half].at[k], grad[half].at[me])

    def home_copy(half, k):
        return direct(2, half, k, ready[half].at[peer(k)], home[half].at[me])

    def line_copy(half, step, axis, k):
        at = (half, step, axis, k)
        held = lines[half].at[axis]
        if step == 0:
            src = dst = held.at[(col, row)[axis]]
            to = along(axis, k)
        else:
            src, dst, to = held, line_place(half, axis), along(1 - axis, k)
        return remote(src, dst, send_line.at[at], recv_line.at[at], to)

    def line_place(half, axis):
        return upd_ref.at[half, axis, (row, col)[axis]]

    loads[0].wait()
    for half in range(2):
        for p in range(HALF):
            staged[half, :, p] = given[block_at[half * HALF + p]]
        if half == 0:
            pl.semaphore_wait(barrier, n - 1)

        @pl.loop(0, n - 1)
        def _(i):
            part_copy(half, turned_round(i)).start()

    @pl.loop(0, n)
    def _(k):
        to = peer(k)
        for half in range(2):
            index = jnp.int32(0)
            for i in range(1, HALF):
                index = jnp.where(owner_at[half * HALF + i] == to, i, index)
            index_at[half, k] = index

    def mine(half, slot):
        tests = []
        for owner, rank, at in zip(owners, ranks, places):
            inside = (at < HALF) if half == 0 else (at >= HALF)
            tests.append((owner == me) & inside & ((rank == 0) if slot == 0 else (rank > 0)))
        return chosen(tests, [1] * blocks) > 0

    def to_owners(half):
        acc[half][...] = staged[half, me].astype(F32)

        @pl.loop(1, n)
        def _(k):
            part_copy(half, k).wait_recv()
            acc[half][...] += parts[half][k].astype(F32)

        @pl.loop(0, n - 1)
        def _(i):
            k = turned_round(i)
            picked[half][k] = acc[half][index_at[half, k]]
            slot_copy(half, k).start()

        grad[half][me] = acc[half][index_at[half, 0]]

    eye = lax.broadcasted_iota(jnp.int32, (width, width), 0) == lax.broadcasted_iota(
        jnp.int32, (width, width), 1
    )

    def solve(half, used, left_old, right_old, beside):
        @pl.loop(1, n)
        def _(k):
            slot_copy(half, k).wait_recv()

        value = jnp.where(used, grad[half][...].reshape(width, width), 0.0)
        plain, turned = split(value), split(value.T)
        left_new = DECAY * left_old + (1.0 - DECAY) * product(plain, turned)
        right_new = DECAY * right_old + (1.0 - DECAY) * product(turned, plain)
        if half == 0:
            left_out[0] = left_new
            right_out[0] = right_new
        else:
            for slot in range(2):
                here = mine(1, slot)
                for out, old, new in (
                    (left_out, left, left_new), (right_out, right, right_new)
                ):
                    rest = out[0] if slot == 0 else DECAY * old[1]
                    out[slot] = jnp.where(here, new, rest)
        first, second = Root(left_new, eye), Root(right_new, eye)
        moved = product(split(product(first.factor, plain)), second.factor)
        for step in range(1, ITERS):
            first.advance()
            second.advance()
            beside(step)
            moved = product(split(product(first.factor, split(moved))), second.factor)
        direction = (first.gain * second.gain) * moved
        count = 1.0 / (width * width)
        ratio = jnp.sqrt(total(value * value) * count) / jnp.sqrt(
            total(direction * direction) * count + 1e-06
        )
        ready[half][...] = (direction * ratio).astype(BF16).reshape(ready[half].shape)

        @pl.loop(0, n - 1)
        def _(i):
            home_copy(half, turned_round(i)).start()

        home[half][me] = ready[half][me]

    def along_first(half):
        @pl.loop(1, n)
        def _(k):
            home_copy(half, k).wait_recv()

        for axis in range(2):
            for p in range(chunk):
                value = home[half][owner_at[half * HALF + axis * chunk + p]]
                lines[half][axis, (col, row)[axis], p] = value
        for i in range(side - 1):
            for axis in range(2):
                line_copy(half, 0, axis, line_turn(axis, i)).start()

    rests = []

    def line_turn(axis, i):
        return 1 + (i + row + col + core + axis) % (side - 1)

    def along_second(half):
        for axis in range(2):
            for k in range(1, side):
                line_copy(half, 0, axis, k).wait_recv()
        for i in range(side - 1):
            for axis in range(2):
                line_copy(half, 1, axis, line_turn(axis, i)).start()
        for axis in range(2):
            rest = pltpu.make_async_copy(
                lines[half].at[axis], line_place(half, axis), local.at[5 + 2 * half + axis]
            )
            rest.start()
            rests.append(rest)

    to_owners(0)
    loads[1].wait()
    loads[2].wait()

    def beside_first(step):
        if step == 2:
            to_owners(1)

    def beside_second(step):
        if step == 3:
            along_first(0)

    solve(0, mine(0, 0), left[0], right[0], beside_first)
    slot = jnp.where(mine(1, 1), 1, 0)
    used = mine(1, 0) | mine(1, 1)
    solve(1, used, left[slot], right[slot], beside_second)
    along_second(0)
    for ref, out, at in ((left_out, ln_ref, 3), (right_out, rn_ref, 4)):
        rest = pltpu.make_async_copy(ref, out, local.at[at])
        rest.start()
        rests.append(rest)
    along_first(1)
    along_second(1)

    @pl.loop(1, n)
    def _(k):
        for half in range(2):
            part_copy(half, k).wait_send()
            slot_copy(half, k).wait_send()
            home_copy(half, k).wait_send()

    for half in range(2):
        for axis in range(2):
            for k in range(1, side):
                line_copy(half, 0, axis, k).wait_send()
                line_copy(half, 1, axis, k).wait()
    for rest in rests:
        rest.wait()


def order_kernel(
    own_ref, upd_ref, ln_ref, rn_ref, out_ref, lo_ref, ro_ref, upd, left, right, whole, into, out
):
    blocks = own_ref.shape[0]
    side, chunk = upd.shape[2], upd.shape[4]
    reads = [
        pltpu.make_async_copy(upd_ref.at[half, axis], upd.at[half, axis], into.at[2 * half + axis])
        for half in range(2)
        for axis in range(2)
    ]
    reads += [
        pltpu.make_async_copy(ln_ref, left, into.at[4]),
        pltpu.make_async_copy(rn_ref, right, into.at[5]),
    ]
    for read in reads:
        read.start()
    _, places = ranks_of([own_ref[b] for b in range(blocks)])
    writes = []
    for p in range(blocks):
        half, axis, i = p // HALF, p % HALF // chunk, p % chunk
        if i == 0:
            reads[2 * half + axis].wait()
        for row in range(side):
            for col in range(side):
                line, at = (row, col) if axis == 0 else (col, row)
                whole[p, row * side + col] = upd[half, axis, line, at, i]
        block = chosen([place == p for place in places], range(blocks))
        writes.append(pltpu.make_async_copy(whole.at[p], out_ref.at[block], out.at[p]))
        writes[-1].start()
    for i, ref, to in ((0, left, lo_ref), (1, right, ro_ref)):
        reads[4 + i].wait()
        writes.append(pltpu.make_async_copy(ref, to, out.at[blocks + i]))
        writes[-1].start()
    for write in writes:
        write.wait()


def local(side, grad_parts, owner_list, left_stats, right_stats):
    n = side * side
    _, blocks, width, _ = grad_parts.shape
    owners = owner_list[:, 0]
    tiles = (blocks, n, ROWS, width)
    pair = (2, width, width)
    vmem = pltpu.VMEM
    anywhere = pl.BlockSpec(memory_space=pl.ANY)
    scalars = pl.BlockSpec(memory_space=pltpu.SMEM)
    piece = (n, ROWS, width)
    gathered = (2, 2, side, side, HALF // 2, ROWS, width)
    shapes = (
        jax.ShapeDtypeStruct(gathered, BF16),
        jax.ShapeDtypeStruct(pair, F32),
        jax.ShapeDtypeStruct(pair, F32),
    )
    some = (HALF, ROWS, width)
    dma = pltpu.SemaphoreType.DMA
    update, left_new, right_new = pl.pallas_call(
        functools.partial(kernel, side),
        out_shape=shapes,
        in_specs=[scalars] + [anywhere] * 3,
        out_specs=(anywhere,) * 3,
        scratch_shapes=[vmem(tiles, BF16), vmem((2, n) + some, BF16)]
        + [vmem((n,) + some, BF16)] * 2
        + [vmem(some, F32)] * 2
        + [vmem(piece, F32)] * 4
        + [vmem(pair, F32)] * 4
        + [vmem(piece, BF16)] * 4
        + [vmem((2, side, HALF // 2, ROWS, width), BF16)] * 2
        + [
            pltpu.SMEM((blocks,), jnp.int32),
            pltpu.SMEM((blocks,), jnp.int32),
            pltpu.SMEM((2, n), jnp.int32),
            dma((6, n)),
            dma((6, n)),
            dma((2, 2, 2, side)),
            dma((2, 2, 2, side)),
            dma((9,)),
        ],
        compiler_params=pltpu.CompilerParams(
            collective_id=0, has_side_effects=True, vmem_limit_bytes=VMEM_BYTES
        ),
    )(
        owners,
        grad_parts.reshape(tiles),
        left_stats.reshape(pair),
        right_stats.reshape(pair),
    )
    update, left_new, right_new = pl.pallas_call(
        order_kernel,
        out_shape=(jax.ShapeDtypeStruct(tiles, BF16),) + shapes[1:],
        in_specs=[scalars] + [anywhere] * 3,
        out_specs=(anywhere,) * 3,
        scratch_shapes=[
            vmem(gathered, BF16),
            vmem(pair, F32),
            vmem(pair, F32),
            vmem(tiles, BF16),
            dma((6,)),
            dma((blocks + 2,)),
        ],
        compiler_params=pltpu.CompilerParams(vmem_limit_bytes=VMEM_BYTES),
    )(owners, update, left_new, right_new)
    return (
        update.reshape(blocks, width, width),
        left_new.reshape(left_stats.shape),
        right_new.reshape(right_stats.shape),
    )


def solution(mesh):
    side = int(round(mesh.shape["dp"] ** 0.5))
    return jax.shard_map(
        functools.partial(local, side),
        mesh=mesh,
        in_specs=(
            P("dp", "shard", None, None),
            P("shard", None),
            P("dp", "shard", None, None, None),
            P("dp", "shard", None, None, None),
        ),
        out_specs=(
            P("shard", None, None),
            P("dp", "shard", None, None, None),
            P("dp", "shard", None, None, None),
        ),
        check_vma=False,
    )
```

```python
import functools

import jax
import jax.numpy as jnp
from jax import lax
from jax.experimental import pallas as pl
from jax.experimental.pallas import tpu as pltpu
from jax.sharding import PartitionSpec as P

ITERS = 4
DECAY = 0.9
RIDGE = 0.01
ROWS = 16
VMEM_BYTES = 56 * 1024 * 1024
HALF = 6
BF16, F32 = jnp.bfloat16, jnp.float32
MESH = pl.DeviceIdType.MESH


def split(value):
    high = value.astype(BF16)
    return high, (value - high.astype(F32)).astype(BF16)


def product(first, second):
    (ah, al), (bh, bl) = first, second
    return jnp.dot(
        jnp.concatenate([ah, ah, al], axis=1),
        jnp.concatenate([bh, bl, bh], axis=0),
        preferred_element_type=F32,
    )


def total(value):
    return jnp.sum(jnp.sum(value, axis=0, keepdims=True), axis=1, keepdims=True)


def ranks_of(owners):
    ranks, places, kinds = [], [], []
    for b, owner in enumerate(owners):
        rank = sum((jnp.where(other == owner, 1, 0) for other in owners[:b]), jnp.int32(0))
        later = sum((jnp.where(other == owner, 1, 0) for other in owners[b + 1 :]), jnp.int32(0))
        ranks.append(rank)
        kinds.append(jnp.where(rank > 0, 2, jnp.where(later > 0, 0, 1)))
    counts = [sum(jnp.where(kind == i, 1, 0) for kind in kinds) for i in range(2)]
    nexts = [jnp.int32(0), counts[0], counts[0] + counts[1]]
    for kind in kinds:
        places.append(jnp.where(kind == 0, nexts[0], jnp.where(kind == 1, nexts[1], nexts[2])))
        nexts = [at + jnp.where(kind == i, 1, 0) for i, at in enumerate(nexts)]
    return ranks, places


def chosen(tests, values):
    return sum(jnp.where(test, value, 0) for test, value in zip(tests, values))


class Root:
    def __init__(self, statistic, eye):
        width = statistic.shape[0]
        shift = total(jnp.where(eye, statistic, 0.0)) * (RIDGE / width)
        shifted = statistic + jnp.where(eye, shift, 0.0)
        scale = 2.5 / jnp.sqrt(total(shifted * shifted) + 1e-06)
        self.eye = eye
        self.gain = jnp.sqrt(jnp.sqrt(scale))
        self.power = scale * shifted
        self.next_factor()

    def next_factor(self):
        self.factor = split(jnp.where(self.eye, 1.25, 0.0) - 0.25 * self.power)

    def advance(self):
        square = split(product(self.factor, self.factor))
        fourth = split(product(square, square))
        self.power = product(fourth, split(self.power))
        self.next_factor()


def kernel(
    side, own_ref, g_ref, ls_ref, rs_ref, upd_ref, ln_ref, rn_ref,
    parts, acc, picked0, picked1, grad0, grad1,
    left, right, left_out, right_out, ready0, ready1, home0, home1, lines0, lines1,
    block_at, owner_at, index_at,
    send, recv, send_line, recv_line, local,
):
    n = side * side
    blocks = own_ref.shape[0]
    width = left.shape[1]
    me = lax.axis_index("dp")
    row, col = me // side, me % side
    chunk = HALF // 2
    picked, grad = (picked0, picked1), (grad0, grad1)
    ready, home, lines = (ready0, ready1), (home0, home1), (lines0, lines1)

    def peer(k):
        return ((row + k // side) % side) * side + (col + k % side) % side

    def along(axis, k):
        if axis == 0:
            return row * side + (col + k) % side
        return ((row + k) % side) * side + col

    core = lax.axis_index("shard") % 2

    def turned_round(i):
        return 1 + (i + me + core * (n // 2 - 1)) % (n - 1)

    loads = [
        pltpu.make_async_copy(g_ref.at[:, me], parts.at[0], local.at[0]),
        pltpu.make_async_copy(ls_ref, left, local.at[1]),
        pltpu.make_async_copy(rs_ref, right, local.at[2]),
    ]
    for load in loads:
        load.start()
    barrier = pltpu.get_barrier_semaphore()

    @pl.loop(1, n)
    def _(k):
        pl.semaphore_signal(barrier, inc=1, device_id={"dp": peer(k)}, device_id_type=MESH)

    def remote(src, dst, sent, landed, to):
        return pltpu.make_async_remote_copy(
            src_ref=src, dst_ref=dst, send_sem=sent, recv_sem=landed,
            device_id={"dp": to}, device_id_type=MESH,
        )

    def direct(what, half, k, src, dst):
        at = (2 * what + half, k)
        return remote(src, dst, send.at[at], recv.at[at], peer(k))

    def part_copy(k):
        return direct(0, 0, k, g_ref.at[:, peer(k)], parts.at[k])

    def slot_copy(half, k):
        return direct(1, half, k, picked[half].at[k], grad[half].at[me])

    def home_copy(half, k):
        return direct(2, half, k, ready[half].at[peer(k)], home[half].at[me])

    def line_copy(half, step, axis, k):
        at = (half, step, axis, k)
        held = lines[half].at[axis]
        if step == 0:
            src = dst = held.at[(col, row)[axis]]
            to = along(axis, k)
        else:
            src, dst, to = held, line_place(half, axis), along(1 - axis, k)
        return remote(src, dst, send_line.at[at], recv_line.at[at], to)

    def line_place(half, axis):
        return upd_ref.at[half, axis, (row, col)[axis]]

    pl.semaphore_wait(barrier, n - 1)

    @pl.loop(0, n - 1)
    def _(i):
        part_copy(turned_round(i)).start()

    owners = [own_ref[b] for b in range(blocks)]
    ranks, places = ranks_of(owners)

    @pl.loop(0, blocks)
    def _(p):
        tests = [at == p for at in places]
        block_at[p] = chosen(tests, range(blocks))
        owner_at[p] = chosen(tests, owners)

    @pl.loop(0, n)
    def _(k):
        to = peer(k)
        for half in range(2):
            index = jnp.int32(0)
            for p in range(half * HALF, (half + 1) * HALF):
                index = jnp.where(owner_at[p] == to, block_at[p], index)
            index_at[half, k] = index

    def mine(half, slot):
        tests = []
        for owner, rank, at in zip(owners, ranks, places):
            inside = (at < HALF) if half == 0 else (at >= HALF)
            tests.append((owner == me) & inside & ((rank == 0) if slot == 0 else (rank > 0)))
        return chosen(tests, [1] * blocks) > 0

    loads[0].wait()
    acc[...] = parts[0].astype(F32)

    @pl.loop(1, n)
    def _(k):
        part_copy(k).wait_recv()
        acc[...] += parts[k].astype(F32)

    for half in range(2):
        @pl.loop(0, n - 1)
        def _(i):
            k = turned_round(i)
            picked[half][k] = acc[index_at[half, k]]
            slot_copy(half, k).start()

        grad[half][me] = acc[index_at[half, 0]]

    eye = lax.broadcasted_iota(jnp.int32, (width, width), 0) == lax.broadcasted_iota(
        jnp.int32, (width, width), 1
    )

    def solve(half, used, left_old, right_old, beside):
        @pl.loop(1, n)
        def _(k):
            slot_copy(half, k).wait_recv()

        value = jnp.where(used, grad[half][...].reshape(width, width), 0.0)
        plain, turned = split(value), split(value.T)
        left_new = DECAY * left_old + (1.0 - DECAY) * product(plain, turned)
        right_new = DECAY * right_old + (1.0 - DECAY) * product(turned, plain)
        if half == 0:
            left_out[0] = left_new
            right_out[0] = right_new
        else:
            for slot in range(2):
                here = mine(1, slot)
                for out, old, new in (
                    (left_out, left, left_new), (right_out, right, right_new)
                ):
                    rest = out[0] if slot == 0 else DECAY * old[1]
                    out[slot] = jnp.where(here, new, rest)
        first, second = Root(left_new, eye), Root(right_new, eye)
        moved = product(split(product(first.factor, plain)), second.factor)
        for step in range(1, ITERS):
            first.advance()
            second.advance()
            beside(step)
            moved = product(split(product(first.factor, split(moved))), second.factor)
        direction = (first.gain * second.gain) * moved
        count = 1.0 / (width * width)
        ratio = jnp.sqrt(total(value * value) * count) / jnp.sqrt(
            total(direction * direction) * count + 1e-06
        )
        ready[half][...] = (direction * ratio).astype(BF16).reshape(ready[half].shape)

        @pl.loop(0, n - 1)
        def _(i):
            home_copy(half, turned_round(i)).start()

        home[half][me] = ready[half][me]

    def along_first(half):
        @pl.loop(1, n)
        def _(k):
            home_copy(half, k).wait_recv()

        for axis in range(2):
            for p in range(chunk):
                value = home[half][owner_at[half * HALF + axis * chunk + p]]
                lines[half][axis, (col, row)[axis], p] = value
        for i in range(side - 1):
            for axis in range(2):
                line_copy(half, 0, axis, line_turn(axis, i)).start()

    rests = []

    def line_turn(axis, i):
        return 1 + (i + row + col + core + axis) % (side - 1)

    def along_second(half):
        for axis in range(2):
            for k in range(1, side):
                line_copy(half, 0, axis, k).wait_recv()
        for i in range(side - 1):
            for axis in range(2):
                line_copy(half, 1, axis, line_turn(axis, i)).start()
        for axis in range(2):
            rest = pltpu.make_async_copy(
                lines[half].at[axis], line_place(half, axis), local.at[5 + 2 * half + axis]
            )
            rest.start()
            rests.append(rest)

    loads[1].wait()
    loads[2].wait()

    def beside_second(step):
        if step == 3:
            along_first(0)

    solve(0, mine(0, 0), left[0], right[0], lambda step: None)
    slot = jnp.where(mine(1, 1), 1, 0)
    used = mine(1, 0) | mine(1, 1)
    solve(1, used, left[slot], right[slot], beside_second)
    along_second(0)
    for ref, out, at in ((left_out, ln_ref, 3), (right_out, rn_ref, 4)):
        rest = pltpu.make_async_copy(ref, out, local.at[at])
        rest.start()
        rests.append(rest)
    along_first(1)
    along_second(1)

    @pl.loop(1, n)
    def _(k):
        part_copy(k).wait_send()
        for half in range(2):
            slot_copy(half, k).wait_send()
            home_copy(half, k).wait_send()

    for half in range(2):
        for axis in range(2):
            for k in range(1, side):
                line_copy(half, 0, axis, k).wait_send()
                line_copy(half, 1, axis, k).wait()
    for rest in rests:
        rest.wait()


def order_kernel(
    own_ref, upd_ref, ln_ref, rn_ref, out_ref, lo_ref, ro_ref, upd, left, right, whole, into, out
):
    blocks = own_ref.shape[0]
    side, chunk = upd.shape[2], upd.shape[4]
    reads = [
        pltpu.make_async_copy(upd_ref.at[half, axis], upd.at[half, axis], into.at[2 * half + axis])
        for half in range(2)
        for axis in range(2)
    ]
    reads += [
        pltpu.make_async_copy(ln_ref, left, into.at[4]),
        pltpu.make_async_copy(rn_ref, right, into.at[5]),
    ]
    for read in reads:
        read.start()
    _, places = ranks_of([own_ref[b] for b in range(blocks)])
    writes = []
    for p in range(blocks):
        half, axis, i = p // HALF, p % HALF // chunk, p % chunk
        if i == 0:
            reads[2 * half + axis].wait()
        for row in range(side):
            for col in range(side):
                line, at = (row, col) if axis == 0 else (col, row)
                whole[p, row * side + col] = upd[half, axis, line, at, i]
        block = chosen([place == p for place in places], range(blocks))
        writes.append(pltpu.make_async_copy(whole.at[p], out_ref.at[block], out.at[p]))
        writes[-1].start()
    for i, ref, to in ((0, left, lo_ref), (1, right, ro_ref)):
        reads[4 + i].wait()
        writes.append(pltpu.make_async_copy(ref, to, out.at[blocks + i]))
        writes[-1].start()
    for write in writes:
        write.wait()


def local(side, grad_parts, owner_list, left_stats, right_stats):
    n = side * side
    _, blocks, width, _ = grad_parts.shape
    owners = owner_list[:, 0]
    tiles = (blocks, n, ROWS, width)
    pair = (2, width, width)
    vmem = pltpu.VMEM
    anywhere = pl.BlockSpec(memory_space=pl.ANY)
    scalars = pl.BlockSpec(memory_space=pltpu.SMEM)
    piece = (n, ROWS, width)
    gathered = (2, 2, side, side, HALF // 2, ROWS, width)
    shapes = (
        jax.ShapeDtypeStruct(gathered, BF16),
        jax.ShapeDtypeStruct(pair, F32),
        jax.ShapeDtypeStruct(pair, F32),
    )
    dma = pltpu.SemaphoreType.DMA
    update, left_new, right_new = pl.pallas_call(
        functools.partial(kernel, side),
        out_shape=shapes,
        in_specs=[scalars] + [anywhere] * 3,
        out_specs=(anywhere,) * 3,
        scratch_shapes=[vmem((n, blocks, ROWS, width), BF16), vmem((blocks, ROWS, width), F32)]
        + [vmem(piece, F32)] * 4
        + [vmem(pair, F32)] * 4
        + [vmem(piece, BF16)] * 4
        + [vmem((2, side, HALF // 2, ROWS, width), BF16)] * 2
        + [
            pltpu.SMEM((blocks,), jnp.int32),
            pltpu.SMEM((blocks,), jnp.int32),
            pltpu.SMEM((2, n), jnp.int32),
            dma((6, n)),
            dma((6, n)),
            dma((2, 2, 2, side)),
            dma((2, 2, 2, side)),
            dma((9,)),
        ],
        compiler_params=pltpu.CompilerParams(
            collective_id=0, has_side_effects=True, vmem_limit_bytes=VMEM_BYTES
        ),
    )(
        owners,
        grad_parts.reshape(tiles),
        left_stats.reshape(pair),
        right_stats.reshape(pair),
    )
    update, left_new, right_new = pl.pallas_call(
        order_kernel,
        out_shape=(jax.ShapeDtypeStruct(tiles, BF16),) + shapes[1:],
        in_specs=[scalars] + [anywhere] * 3,
        out_specs=(anywhere,) * 3,
        scratch_shapes=[
            vmem(gathered, BF16),
            vmem(pair, F32),
            vmem(pair, F32),
            vmem(tiles, BF16),
            dma((6,)),
            dma((blocks + 2,)),
        ],
        compiler_params=pltpu.CompilerParams(vmem_limit_bytes=VMEM_BYTES),
    )(owners, update, left_new, right_new)
    return (
        update.reshape(blocks, width, width),
        left_new.reshape(left_stats.shape),
        right_new.reshape(right_stats.shape),
    )


def solution(mesh):
    side = int(round(mesh.shape["dp"] ** 0.5))
    return jax.shard_map(
        functools.partial(local, side),
        mesh=mesh,
        in_specs=(
            P("dp", "shard", None, None),
            P("shard", None),
            P("dp", "shard", None, None, None),
            P("dp", "shard", None, None, None),
        ),
        out_specs=(
            P("shard", None, None),
            P("dp", "shard", None, None, None),
            P("dp", "shard", None, None, None),
        ),
        check_vma=False,
    )
```

```python
import functools

import jax
import jax.numpy as jnp
from jax import lax
from jax.experimental import pallas as pl
from jax.experimental.pallas import tpu as pltpu
from jax.sharding import PartitionSpec as P

ITERS = 4
DECAY = 0.9
RIDGE = 0.01
ROWS = 16
VMEM_BYTES = 56 * 1024 * 1024
HALF = 6
BF16, F32 = jnp.bfloat16, jnp.float32
MESH = pl.DeviceIdType.MESH


def split(value):
    high = value.astype(BF16)
    return high, (value - high.astype(F32)).astype(BF16)


def product(first, second):
    (ah, al), (bh, bl) = first, second
    return jnp.dot(
        jnp.concatenate([ah, ah, al], axis=1),
        jnp.concatenate([bh, bl, bh], axis=0),
        preferred_element_type=F32,
    )


def total(value):
    return jnp.sum(jnp.sum(value, axis=0, keepdims=True), axis=1, keepdims=True)


def ranks_of(owners):
    ranks, places, kinds = [], [], []
    for b, owner in enumerate(owners):
        rank = sum((jnp.where(other == owner, 1, 0) for other in owners[:b]), jnp.int32(0))
        later = sum((jnp.where(other == owner, 1, 0) for other in owners[b + 1 :]), jnp.int32(0))
        ranks.append(rank)
        kinds.append(jnp.where(rank > 0, 2, jnp.where(later > 0, 0, 1)))
    counts = [sum(jnp.where(kind == i, 1, 0) for kind in kinds) for i in range(2)]
    nexts = [jnp.int32(0), counts[0], counts[0] + counts[1]]
    for kind in kinds:
        places.append(jnp.where(kind == 0, nexts[0], jnp.where(kind == 1, nexts[1], nexts[2])))
        nexts = [at + jnp.where(kind == i, 1, 0) for i, at in enumerate(nexts)]
    return ranks, places


def chosen(tests, values):
    return sum(jnp.where(test, value, 0) for test, value in zip(tests, values))


class Root:
    def __init__(self, statistic, eye):
        width = statistic.shape[0]
        shift = total(jnp.where(eye, statistic, 0.0)) * (RIDGE / width)
        shifted = statistic + jnp.where(eye, shift, 0.0)
        scale = 2.5 / jnp.sqrt(total(shifted * shifted) + 1e-06)
        self.eye = eye
        self.gain = jnp.sqrt(jnp.sqrt(scale))
        self.power = scale * shifted
        self.next_factor()

    def next_factor(self):
        self.factor = split(jnp.where(self.eye, 1.25, 0.0) - 0.25 * self.power)


def kernel(
    side, own_ref, g_ref, ls_ref, rs_ref, upd_ref, ln_ref, rn_ref,
    parts, acc, picked0, picked1, grad0, grad1,
    left, right, left_out, right_out, ready0, ready1, home0, home1, lines0, lines1,
    block_at, owner_at, index_at,
    send, recv, send_line, recv_line, local,
):
    n = side * side
    blocks = own_ref.shape[0]
    width = left.shape[1]
    me = lax.axis_index("dp")
    row, col = me // side, me % side
    chunk = HALF // 2
    picked, grad = (picked0, picked1), (grad0, grad1)
    ready, home, lines = (ready0, ready1), (home0, home1), (lines0, lines1)

    def peer(k):
        return ((row + k // side) % side) * side + (col + k % side) % side

    def along(axis, k):
        if axis == 0:
            return row * side + (col + k) % side
        return ((row + k) % side) * side + col

    core = lax.axis_index("shard") % 2

    def turned_round(i):
        return 1 + (i + me + core * (n // 2 - 1)) % (n - 1)

    loads = [
        pltpu.make_async_copy(g_ref.at[:, me], parts.at[0], local.at[0]),
        pltpu.make_async_copy(ls_ref, left, local.at[1]),
        pltpu.make_async_copy(rs_ref, right, local.at[2]),
    ]
    for load in loads:
        load.start()
    barrier = pltpu.get_barrier_semaphore()

    @pl.loop(1, n)
    def _(k):
        pl.semaphore_signal(barrier, inc=1, device_id={"dp": peer(k)}, device_id_type=MESH)

    def remote(src, dst, sent, landed, to):
        return pltpu.make_async_remote_copy(
            src_ref=src, dst_ref=dst, send_sem=sent, recv_sem=landed,
            device_id={"dp": to}, device_id_type=MESH,
        )

    def direct(what, half, k, src, dst):
        at = (2 * what + half, k)
        return remote(src, dst, send.at[at], recv.at[at], peer(k))

    def part_copy(k):
        return direct(0, 0, k, g_ref.at[:, peer(k)], parts.at[k])

    def slot_copy(half, k):
        return direct(1, half, k, picked[half].at[k], grad[half].at[me])

    def home_copy(half, k):
        return direct(2, half, k, ready[half].at[peer(k)], home[half].at[me])

    def line_copy(half, step, axis, k):
        at = (half, step, axis, k)
        held = lines[half].at[axis]
        if step == 0:
            src = dst = held.at[(col, row)[axis]]
            to = along(axis, k)
        else:
            src, dst, to = held, line_place(half, axis), along(1 - axis, k)
        return remote(src, dst, send_line.at[at], recv_line.at[at], to)

    def line_place(half, axis):
        return upd_ref.at[half, axis, (row, col)[axis]]

    pl.semaphore_wait(barrier, n - 1)

    @pl.loop(0, n - 1)
    def _(i):
        part_copy(turned_round(i)).start()

    owners = [own_ref[b] for b in range(blocks)]
    ranks, places = ranks_of(owners)

    @pl.loop(0, blocks)
    def _(p):
        tests = [at == p for at in places]
        block_at[p] = chosen(tests, range(blocks))
        owner_at[p] = chosen(tests, owners)

    @pl.loop(0, n)
    def _(k):
        to = peer(k)
        for half in range(2):
            index = jnp.int32(0)
            for p in range(half * HALF, (half + 1) * HALF):
                index = jnp.where(owner_at[p] == to, block_at[p], index)
            index_at[half, k] = index

    def mine(half, slot):
        tests = []
        for owner, rank, at in zip(owners, ranks, places):
            inside = (at < HALF) if half == 0 else (at >= HALF)
            tests.append((owner == me) & inside & ((rank == 0) if slot == 0 else (rank > 0)))
        return chosen(tests, [1] * blocks) > 0

    loads[0].wait()
    acc[...] = parts[0].astype(F32)

    @pl.loop(1, n)
    def _(k):
        part_copy(k).wait_recv()
        acc[...] += parts[k].astype(F32)

    for half in range(2):
        @pl.loop(0, n - 1)
        def _(i):
            k = turned_round(i)
            picked[half][k] = acc[index_at[half, k]]
            slot_copy(half, k).start()

        grad[half][me] = acc[index_at[half, 0]]

    eye = lax.broadcasted_iota(jnp.int32, (width, width), 0) == lax.broadcasted_iota(
        jnp.int32, (width, width), 1
    )

    def solve(half, used, left_old, right_old, beside):
        @pl.loop(1, n)
        def _(k):
            slot_copy(half, k).wait_recv()

        value = jnp.where(used, grad[half][...].reshape(width, width), 0.0)
        plain, turned = split(value), split(value.T)
        left_new = DECAY * left_old + (1.0 - DECAY) * product(plain, turned)
        right_new = DECAY * right_old + (1.0 - DECAY) * product(turned, plain)
        if half == 0:
            left_out[0] = left_new
            right_out[0] = right_new
        else:
            for slot in range(2):
                here = mine(1, slot)
                for out, old, new in (
                    (left_out, left, left_new), (right_out, right, right_new)
                ):
                    rest = out[0] if slot == 0 else DECAY * old[1]
                    out[slot] = jnp.where(here, new, rest)
        count = 1.0 / (width * width)
        size = jnp.sqrt(total(value * value) * count)
        first, second = roots = Root(left_new, eye), Root(right_new, eye)
        moved = plain
        for step in range(1, ITERS):
            squares = [product(root.factor, root.factor) for root in roots]
            half_way = product(first.factor, moved)
            squares = [split(square) for square in squares]
            half_way = split(half_way)
            fourths = [product(square, square) for square in squares]
            moved = product(half_way, second.factor)
            fourths = [split(fourth) for fourth in fourths]
            powers = [split(root.power) for root in roots]
            moved = split(moved)
            for root, fourth, power in zip(roots, fourths, powers):
                root.power = product(fourth, power)
            for root in roots:
                root.next_factor()
            beside(step)
        moved = product(split(product(first.factor, moved)), second.factor)
        gain = first.gain * second.gain
        ratio = size / jnp.sqrt(gain * gain * total(moved * moved) * count + 1e-06)
        ready[half][...] = (moved * (gain * ratio)).astype(BF16).reshape(ready[half].shape)

        @pl.loop(0, n - 1)
        def _(i):
            home_copy(half, turned_round(i)).start()

        home[half][me] = ready[half][me]

    def along_first(half):
        @pl.loop(1, n)
        def _(k):
            home_copy(half, k).wait_recv()

        for axis in range(2):
            for p in range(chunk):
                value = home[half][owner_at[half * HALF + axis * chunk + p]]
                lines[half][axis, (col, row)[axis], p] = value
        for i in range(side - 1):
            for axis in range(2):
                line_copy(half, 0, axis, line_turn(axis, i)).start()

    rests = []

    def line_turn(axis, i):
        return 1 + (i + row + col + core + axis) % (side - 1)

    def along_second(half):
        for axis in range(2):
            for k in range(1, side):
                line_copy(half, 0, axis, k).wait_recv()
        for i in range(side - 1):
            for axis in range(2):
                line_copy(half, 1, axis, line_turn(axis, i)).start()
        for axis in range(2):
            rest = pltpu.make_async_copy(
                lines[half].at[axis], line_place(half, axis), local.at[5 + 2 * half + axis]
            )
            rest.start()
            rests.append(rest)

    loads[1].wait()
    loads[2].wait()

    def beside_second(step):
        if step == 3:
            along_first(0)

    solve(0, mine(0, 0), left[0], right[0], lambda step: None)
    slot = jnp.where(mine(1, 1), 1, 0)
    used = mine(1, 0) | mine(1, 1)
    solve(1, used, left[slot], right[slot], beside_second)
    along_second(0)
    for ref, out, at in ((left_out, ln_ref, 3), (right_out, rn_ref, 4)):
        rest = pltpu.make_async_copy(ref, out, local.at[at])
        rest.start()
        rests.append(rest)
    along_first(1)
    along_second(1)

    @pl.loop(1, n)
    def _(k):
        part_copy(k).wait_send()
        for half in range(2):
            slot_copy(half, k).wait_send()
            home_copy(half, k).wait_send()

    for half in range(2):
        for axis in range(2):
            for k in range(1, side):
                line_copy(half, 0, axis, k).wait_send()
                line_copy(half, 1, axis, k).wait()
    for rest in rests:
        rest.wait()


def order_kernel(
    own_ref, upd_ref, ln_ref, rn_ref, out_ref, lo_ref, ro_ref, upd, left, right, whole, into, out
):
    blocks = own_ref.shape[0]
    side, chunk = upd.shape[2], upd.shape[4]
    reads = [
        pltpu.make_async_copy(upd_ref.at[half, axis], upd.at[half, axis], into.at[2 * half + axis])
        for half in range(2)
        for axis in range(2)
    ]
    reads += [
        pltpu.make_async_copy(ln_ref, left, into.at[4]),
        pltpu.make_async_copy(rn_ref, right, into.at[5]),
    ]
    for read in reads:
        read.start()
    _, places = ranks_of([own_ref[b] for b in range(blocks)])
    writes = []
    for p in range(blocks):
        half, axis, i = p // HALF, p % HALF // chunk, p % chunk
        if i == 0:
            reads[2 * half + axis].wait()
        for row in range(side):
            for col in range(side):
                line, at = (row, col) if axis == 0 else (col, row)
                whole[p, row * side + col] = upd[half, axis, line, at, i]
        block = chosen([place == p for place in places], range(blocks))
        writes.append(pltpu.make_async_copy(whole.at[p], out_ref.at[block], out.at[p]))
        writes[-1].start()
    for i, ref, to in ((0, left, lo_ref), (1, right, ro_ref)):
        reads[4 + i].wait()
        writes.append(pltpu.make_async_copy(ref, to, out.at[blocks + i]))
        writes[-1].start()
    for write in writes:
        write.wait()


def local(side, grad_parts, owner_list, left_stats, right_stats):
    n = side * side
    _, blocks, width, _ = grad_parts.shape
    owners = owner_list[:, 0]
    tiles = (blocks, n, ROWS, width)
    pair = (2, width, width)
    vmem = pltpu.VMEM
    anywhere = pl.BlockSpec(memory_space=pl.ANY)
    scalars = pl.BlockSpec(memory_space=pltpu.SMEM)
    piece = (n, ROWS, width)
    gathered = (2, 2, side, side, HALF // 2, ROWS, width)
    shapes = (
        jax.ShapeDtypeStruct(gathered, BF16),
        jax.ShapeDtypeStruct(pair, F32),
        jax.ShapeDtypeStruct(pair, F32),
    )
    dma = pltpu.SemaphoreType.DMA
    update, left_new, right_new = pl.pallas_call(
        functools.partial(kernel, side),
        out_shape=shapes,
        in_specs=[scalars] + [anywhere] * 3,
        out_specs=(anywhere,) * 3,
        scratch_shapes=[vmem((n, blocks, ROWS, width), BF16), vmem((blocks, ROWS, width), F32)]
        + [vmem(piece, F32)] * 4
        + [vmem(pair, F32)] * 4
        + [vmem(piece, BF16)] * 4
        + [vmem((2, side, HALF // 2, ROWS, width), BF16)] * 2
        + [
            pltpu.SMEM((blocks,), jnp.int32),
            pltpu.SMEM((blocks,), jnp.int32),
            pltpu.SMEM((2, n), jnp.int32),
            dma((6, n)),
            dma((6, n)),
            dma((2, 2, 2, side)),
            dma((2, 2, 2, side)),
            dma((9,)),
        ],
        compiler_params=pltpu.CompilerParams(
            collective_id=0, has_side_effects=True, vmem_limit_bytes=VMEM_BYTES
        ),
    )(
        owners,
        grad_parts.reshape(tiles),
        left_stats.reshape(pair),
        right_stats.reshape(pair),
    )
    update, left_new, right_new = pl.pallas_call(
        order_kernel,
        out_shape=(jax.ShapeDtypeStruct(tiles, BF16),) + shapes[1:],
        in_specs=[scalars] + [anywhere] * 3,
        out_specs=(anywhere,) * 3,
        scratch_shapes=[
            vmem(gathered, BF16),
            vmem(pair, F32),
            vmem(pair, F32),
            vmem(tiles, BF16),
            dma((6,)),
            dma((blocks + 2,)),
        ],
        compiler_params=pltpu.CompilerParams(vmem_limit_bytes=VMEM_BYTES),
    )(owners, update, left_new, right_new)
    return (
        update.reshape(blocks, width, width),
        left_new.reshape(left_stats.shape),
        right_new.reshape(right_stats.shape),
    )


def solution(mesh):
    side = int(round(mesh.shape["dp"] ** 0.5))
    return jax.shard_map(
        functools.partial(local, side),
        mesh=mesh,
        in_specs=(
            P("dp", "shard", None, None),
            P("shard", None),
            P("dp", "shard", None, None, None),
            P("dp", "shard", None, None, None),
        ),
        out_specs=(
            P("shard", None, None),
            P("dp", "shard", None, None, None),
            P("dp", "shard", None, None, None),
        ),
        check_vma=False,
    )
```

```python
import functools

import jax
import jax.numpy as jnp
from jax import lax
from jax.experimental import pallas as pl
from jax.experimental.pallas import tpu as pltpu
from jax.sharding import PartitionSpec as P

ITERS = 4
DECAY = 0.9
RIDGE = 0.01
ROWS = 16
VMEM_BYTES = 56 * 1024 * 1024
HALF = 6
BF16, F32 = jnp.bfloat16, jnp.float32
MESH = pl.DeviceIdType.MESH


def split(value):
    high = value.astype(BF16)
    return high, (value - high.astype(F32)).astype(BF16)


def product(first, second):
    (ah, al), (bh, bl) = first, second
    return jnp.dot(
        jnp.concatenate([ah, ah, al], axis=1),
        jnp.concatenate([bh, bl, bh], axis=0),
        preferred_element_type=F32,
    )


def total(value):
    return jnp.sum(jnp.sum(value, axis=0, keepdims=True), axis=1, keepdims=True)


def ranks_of(owners):
    ranks, places, kinds = [], [], []
    for b, owner in enumerate(owners):
        rank = sum((jnp.where(other == owner, 1, 0) for other in owners[:b]), jnp.int32(0))
        later = sum((jnp.where(other == owner, 1, 0) for other in owners[b + 1 :]), jnp.int32(0))
        ranks.append(rank)
        kinds.append(jnp.where(rank > 0, 2, jnp.where(later > 0, 0, 1)))
    counts = [sum(jnp.where(kind == i, 1, 0) for kind in kinds) for i in range(2)]
    nexts = [jnp.int32(0), counts[0], counts[0] + counts[1]]
    for kind in kinds:
        places.append(jnp.where(kind == 0, nexts[0], jnp.where(kind == 1, nexts[1], nexts[2])))
        nexts = [at + jnp.where(kind == i, 1, 0) for i, at in enumerate(nexts)]
    return ranks, places


def chosen(tests, values):
    return sum(jnp.where(test, value, 0) for test, value in zip(tests, values))


class Root:
    def __init__(self, statistic, eye):
        width = statistic.shape[0]
        shift = total(jnp.where(eye, statistic, 0.0)) * (RIDGE / width)
        shifted = statistic + jnp.where(eye, shift, 0.0)
        scale = 2.5 / jnp.sqrt(total(shifted * shifted) + 1e-06)
        self.eye = eye
        self.gain = jnp.sqrt(jnp.sqrt(scale))
        self.power = scale * shifted
        self.next_factor()

    def next_factor(self):
        self.factor = split(jnp.where(self.eye, 1.25, 0.0) - 0.25 * self.power)


def kernel(
    side, own_ref, g_ref, ls_ref, rs_ref, upd_ref, ln_ref, rn_ref,
    parts, sums, second_sums, acc, picked0, picked1, grad0, grad1,
    left, right, left_out, right_out, ready0, ready1, home0, home1, lines0, lines1,
    block_at, owner_at, index_at, send_sum, recv_sum,
    send, recv, send_line, recv_line, local,
):
    n = side * side
    blocks = own_ref.shape[0]
    width = left.shape[1]
    me = lax.axis_index("dp")
    row, col = me // side, me % side
    chunk = HALF // 2
    picked, grad = (picked0, picked1), (grad0, grad1)
    ready, home, lines = (ready0, ready1), (home0, home1), (lines0, lines1)

    def peer(k):
        return ((row + k // side) % side) * side + (col + k % side) % side

    def along(axis, k):
        if axis == 0:
            return row * side + (col + k) % side
        return ((row + k) % side) * side + col

    core = lax.axis_index("shard") % 2

    def turned_round(i):
        return 1 + (i + me + core * (n // 2 - 1)) % (n - 1)

    loads = [
        pltpu.make_async_copy(ls_ref, left, local.at[1]),
        pltpu.make_async_copy(rs_ref, right, local.at[2]),
    ]
    pieces = [(j, kind) for j in range(2) for kind in range(2)]
    for j, kind in pieces:
        loads.append(
            pltpu.make_async_copy(
                g_ref.at[pl.ds(kind * HALF + j * chunk, chunk), (col, row)[kind]],
                parts.at[kind, j, 0],
                local.at[9 + 2 * j + kind],
            )
        )
    for load in loads:
        load.start()
    barrier = pltpu.get_barrier_semaphore()

    @pl.loop(1, n)
    def _(k):
        pl.semaphore_signal(barrier, inc=1, device_id={"dp": peer(k)}, device_id_type=MESH)

    def remote(src, dst, sent, landed, to):
        return pltpu.make_async_remote_copy(
            src_ref=src, dst_ref=dst, send_sem=sent, recv_sem=landed,
            device_id={"dp": to}, device_id_type=MESH,
        )

    def direct(what, half, k, src, dst):
        at = (2 * what + half, k)
        return remote(src, dst, send.at[at], recv.at[at], peer(k))

    def part_copy(j, kind, k):
        src = g_ref.at[pl.ds(kind * HALF + j * chunk, chunk), ((col, row)[kind] + k) % side]
        at = (0, kind, j, k)
        return remote(
            src, parts.at[kind, j, k], send_sum.at[at], recv_sum.at[at], along(kind, k)
        )

    def sum_copy(j, kind, k):
        src = sums.at[kind, j, ((row, col)[kind] + k) % side]
        at = (1, kind, j, k)
        return remote(
            src, second_sums.at[kind, j, k], send_sum.at[at], recv_sum.at[at], along(1 - kind, k)
        )

    def slot_copy(half, k):
        return direct(1, half, k, picked[half].at[k], grad[half].at[me])

    def home_copy(half, k):
        return direct(2, half, k, ready[half].at[peer(k)], home[half].at[me])

    def line_copy(half, step, axis, k):
        at = (half, step, axis, k)
        held = lines[half].at[axis]
        if step == 0:
            src = dst = held.at[(col, row)[axis]]
            to = along(axis, k)
        else:
            src, dst, to = held, line_place(half, axis), along(1 - axis, k)
        return remote(src, dst, send_line.at[at], recv_line.at[at], to)

    def line_place(half, axis):
        return upd_ref.at[half, axis, (row, col)[axis]]

    pl.semaphore_wait(barrier, n - 1)

    for j in range(2):
        for i in range(1, side):
            for kind in range(2):
                part_copy(j, kind, i).start()

    owners = [own_ref[b] for b in range(blocks)]
    ranks, places = ranks_of(owners)

    @pl.loop(0, blocks)
    def _(p):
        tests = [at == p for at in places]
        block_at[p] = chosen(tests, range(blocks))
        owner_at[p] = chosen(tests, owners)

    @pl.loop(0, n)
    def _(k):
        to = peer(k)
        for half in range(2):
            index = jnp.int32(0)
            for p in range(half * HALF, (half + 1) * HALF):
                index = jnp.where(owner_at[p] == to, block_at[p], index)
            index_at[half, k] = index

    def mine(half, slot):
        tests = []
        for owner, rank, at in zip(owners, ranks, places):
            inside = (at < HALF) if half == 0 else (at >= HALF)
            tests.append((owner == me) & inside & ((rank == 0) if slot == 0 else (rank > 0)))
        return chosen(tests, [1] * blocks) > 0

    for number, (j, kind) in enumerate(pieces):
        loads[2 + number].wait()
        for k in range(1, side):
            part_copy(j, kind, k).wait_recv()

        @pl.loop(0, side)
        def _(v):
            sums[kind, j, v] = sum(parts[kind, j, k, :, v].astype(F32) for k in range(side))

        for k in range(1, side):
            sum_copy(j, kind, k).start()
    for j, kind in pieces:
        for k in range(1, side):
            sum_copy(j, kind, k).wait_recv()
        acc[pl.ds(kind * HALF + j * chunk, chunk)] = sums[kind, j, (row, col)[kind]] + (
            second_sums[kind, j, 1] + second_sums[kind, j, 2] + second_sums[kind, j, 3]
        )

    for half in range(2):
        @pl.loop(0, n - 1)
        def _(i):
            k = turned_round(i)
            picked[half][k] = acc[index_at[half, k]]
            slot_copy(half, k).start()

        grad[half][me] = acc[index_at[half, 0]]

    def low_mine(half):
        tests = []
        for owner, at in zip(owners[:HALF], places[:HALF]):
            tests.append((owner == me) & ((at < HALF) if half == 0 else (at >= HALF)))
        return chosen(tests, [1] * HALF) > 0

    eye = lax.broadcasted_iota(jnp.int32, (width, width), 0) == lax.broadcasted_iota(
        jnp.int32, (width, width), 1
    )

    def solve(half, used, left_old, right_old, beside):
        @pl.loop(1, n)
        def _(k):
            slot_copy(half, k).wait_recv()

        across = jnp.stack([grad[half][(i % side) * side + i // side] for i in range(n)])
        value = jnp.where(low_mine(half), across, grad[half][...]).reshape(width, width)
        value = jnp.where(used, value, 0.0)
        plain, turned = split(value), split(value.T)
        left_new = DECAY * left_old + (1.0 - DECAY) * product(plain, turned)
        right_new = DECAY * right_old + (1.0 - DECAY) * product(turned, plain)
        if half == 0:
            left_out[0] = left_new
            right_out[0] = right_new
        else:
            for slot in range(2):
                here = mine(1, slot)
                for out, old, new in (
                    (left_out, left, left_new), (right_out, right, right_new)
                ):
                    rest = out[0] if slot == 0 else DECAY * old[1]
                    out[slot] = jnp.where(here, new, rest)
        count = 1.0 / (width * width)
        size = jnp.sqrt(total(value * value) * count)
        first, second = roots = Root(left_new, eye), Root(right_new, eye)
        moved = plain
        for step in range(1, ITERS):
            squares = [product(root.factor, root.factor) for root in roots]
            half_way = product(first.factor, moved)
            squares = [split(square) for square in squares]
            half_way = split(half_way)
            fourths = [product(square, square) for square in squares]
            moved = product(half_way, second.factor)
            fourths = [split(fourth) for fourth in fourths]
            powers = [split(root.power) for root in roots]
            moved = split(moved)
            for root, fourth, power in zip(roots, fourths, powers):
                root.power = product(fourth, power)
            for root in roots:
                root.next_factor()
            beside(step)
        moved = product(split(product(first.factor, moved)), second.factor)
        gain = first.gain * second.gain
        ratio = size / jnp.sqrt(gain * gain * total(moved * moved) * count + 1e-06)
        ready[half][...] = (moved * (gain * ratio)).astype(BF16).reshape(ready[half].shape)

        @pl.loop(0, n - 1)
        def _(i):
            home_copy(half, turned_round(i)).start()

        home[half][me] = ready[half][me]

    def along_first(half):
        @pl.loop(1, n)
        def _(k):
            home_copy(half, k).wait_recv()

        for axis in range(2):
            for p in range(chunk):
                value = home[half][owner_at[half * HALF + axis * chunk + p]]
                lines[half][axis, (col, row)[axis], p] = value
        for i in range(side - 1):
            for axis in range(2):
                line_copy(half, 0, axis, line_turn(axis, i)).start()

    rests = []

    def line_turn(axis, i):
        return 1 + (i + row + col + core + axis) % (side - 1)

    def along_second(half):
        for axis in range(2):
            for k in range(1, side):
                line_copy(half, 0, axis, k).wait_recv()
        for i in range(side - 1):
            for axis in range(2):
                line_copy(half, 1, axis, line_turn(axis, i)).start()
        for axis in range(2):
            rest = pltpu.make_async_copy(
                lines[half].at[axis], line_place(half, axis), local.at[5 + 2 * half + axis]
            )
            rest.start()
            rests.append(rest)

    loads[0].wait()
    loads[1].wait()

    def beside_second(step):
        if step == 3:
            along_first(0)

    solve(0, mine(0, 0), left[0], right[0], lambda step: None)
    slot = jnp.where(mine(1, 1), 1, 0)
    used = mine(1, 0) | mine(1, 1)
    solve(1, used, left[slot], right[slot], beside_second)
    along_second(0)
    for ref, out, at in ((left_out, ln_ref, 3), (right_out, rn_ref, 4)):
        rest = pltpu.make_async_copy(ref, out, local.at[at])
        rest.start()
        rests.append(rest)
    along_first(1)
    along_second(1)

    @pl.loop(1, n)
    def _(k):
        for half in range(2):
            slot_copy(half, k).wait_send()
            home_copy(half, k).wait_send()

    for j, kind in pieces:
        for k in range(1, side):
            part_copy(j, kind, k).wait_send()
            sum_copy(j, kind, k).wait_send()
    for half in range(2):
        for axis in range(2):
            for k in range(1, side):
                line_copy(half, 0, axis, k).wait_send()
                line_copy(half, 1, axis, k).wait()
    for rest in rests:
        rest.wait()


def order_kernel(
    own_ref, upd_ref, ln_ref, rn_ref, out_ref, lo_ref, ro_ref, upd, left, right, whole, into, out
):
    blocks = own_ref.shape[0]
    side, chunk = upd.shape[2], upd.shape[4]
    reads = [
        pltpu.make_async_copy(upd_ref.at[half, axis], upd.at[half, axis], into.at[2 * half + axis])
        for half in range(2)
        for axis in range(2)
    ]
    reads += [
        pltpu.make_async_copy(ln_ref, left, into.at[4]),
        pltpu.make_async_copy(rn_ref, right, into.at[5]),
    ]
    for read in reads:
        read.start()
    _, places = ranks_of([own_ref[b] for b in range(blocks)])
    writes = []
    for p in range(blocks):
        half, axis, i = p // HALF, p % HALF // chunk, p % chunk
        if i == 0:
            reads[2 * half + axis].wait()
        for row in range(side):
            for col in range(side):
                line, at = (row, col) if axis == 0 else (col, row)
                whole[p, row * side + col] = upd[half, axis, line, at, i]
        block = chosen([place == p for place in places], range(blocks))
        writes.append(pltpu.make_async_copy(whole.at[p], out_ref.at[block], out.at[p]))
        writes[-1].start()
    for i, ref, to in ((0, left, lo_ref), (1, right, ro_ref)):
        reads[4 + i].wait()
        writes.append(pltpu.make_async_copy(ref, to, out.at[blocks + i]))
        writes[-1].start()
    for write in writes:
        write.wait()


def local(side, grad_parts, owner_list, left_stats, right_stats):
    n = side * side
    _, blocks, width, _ = grad_parts.shape
    owners = owner_list[:, 0]
    tiles = (blocks, n, ROWS, width)
    pair = (2, width, width)
    vmem = pltpu.VMEM
    anywhere = pl.BlockSpec(memory_space=pl.ANY)
    scalars = pl.BlockSpec(memory_space=pltpu.SMEM)
    piece = (n, ROWS, width)
    gathered = (2, 2, side, side, HALF // 2, ROWS, width)
    shapes = (
        jax.ShapeDtypeStruct(gathered, BF16),
        jax.ShapeDtypeStruct(pair, F32),
        jax.ShapeDtypeStruct(pair, F32),
    )
    dma = pltpu.SemaphoreType.DMA
    update, left_new, right_new = pl.pallas_call(
        functools.partial(kernel, side),
        out_shape=shapes,
        in_specs=[scalars] + [anywhere] * 3,
        out_specs=(anywhere,) * 3,
        scratch_shapes=[
            vmem((2, 2, side, HALF // 2, side, ROWS, width), BF16),
            vmem((2, 2, side, HALF // 2, ROWS, width), F32),
            vmem((2, 2, side, HALF // 2, ROWS, width), F32),
            vmem((blocks, ROWS, width), F32),
        ]
        + [vmem(piece, F32)] * 4
        + [vmem(pair, F32)] * 4
        + [vmem(piece, BF16)] * 4
        + [vmem((2, side, HALF // 2, ROWS, width), BF16)] * 2
        + [
            pltpu.SMEM((blocks,), jnp.int32),
            pltpu.SMEM((blocks,), jnp.int32),
            pltpu.SMEM((2, n), jnp.int32),
            dma((2, 2, 2, side)),
            dma((2, 2, 2, side)),
            dma((6, n)),
            dma((6, n)),
            dma((2, 2, 2, side)),
            dma((2, 2, 2, side)),
            dma((13,)),
        ],
        compiler_params=pltpu.CompilerParams(
            collective_id=0, has_side_effects=True, vmem_limit_bytes=VMEM_BYTES
        ),
    )(
        owners,
        grad_parts.reshape(blocks, side, side, ROWS, width),
        left_stats.reshape(pair),
        right_stats.reshape(pair),
    )
    update, left_new, right_new = pl.pallas_call(
        order_kernel,
        out_shape=(jax.ShapeDtypeStruct(tiles, BF16),) + shapes[1:],
        in_specs=[scalars] + [anywhere] * 3,
        out_specs=(anywhere,) * 3,
        scratch_shapes=[
            vmem(gathered, BF16),
            vmem(pair, F32),
            vmem(pair, F32),
            vmem(tiles, BF16),
            dma((6,)),
            dma((blocks + 2,)),
        ],
        compiler_params=pltpu.CompilerParams(vmem_limit_bytes=VMEM_BYTES),
    )(owners, update, left_new, right_new)
    return (
        update.reshape(blocks, width, width),
        left_new.reshape(left_stats.shape),
        right_new.reshape(right_stats.shape),
    )


def solution(mesh):
    side = int(round(mesh.shape["dp"] ** 0.5))
    return jax.shard_map(
        functools.partial(local, side),
        mesh=mesh,
        in_specs=(
            P("dp", "shard", None, None),
            P("shard", None),
            P("dp", "shard", None, None, None),
            P("dp", "shard", None, None, None),
        ),
        out_specs=(
            P("shard", None, None),
            P("dp", "shard", None, None, None),
            P("dp", "shard", None, None, None),
        ),
        check_vma=False,
    )
```

```python
import functools

import jax
import jax.numpy as jnp
from jax import lax
from jax.experimental import pallas as pl
from jax.experimental.pallas import tpu as pltpu
from jax.sharding import PartitionSpec as P

ITERS = 4
DECAY = 0.9
RIDGE = 0.01
ROWS = 16
VMEM_BYTES = 56 * 1024 * 1024
FAR_FIRST = (2, 1, 3)
HALF = 6
BF16, F32 = jnp.bfloat16, jnp.float32
MESH = pl.DeviceIdType.MESH


def split(value):
    high = value.astype(BF16)
    return high, (value - high.astype(F32)).astype(BF16)


def product(first, second):
    (ah, al), (bh, bl) = first, second
    return jnp.dot(
        jnp.concatenate([ah, ah, al], axis=1),
        jnp.concatenate([bh, bl, bh], axis=0),
        preferred_element_type=F32,
    )


def total(value):
    return jnp.sum(jnp.sum(value, axis=0, keepdims=True), axis=1, keepdims=True)


def ranks_of(owners):
    ranks, places, kinds = [], [], []
    for b, owner in enumerate(owners):
        rank = sum((jnp.where(other == owner, 1, 0) for other in owners[:b]), jnp.int32(0))
        later = sum((jnp.where(other == owner, 1, 0) for other in owners[b + 1 :]), jnp.int32(0))
        ranks.append(rank)
        kinds.append(jnp.where(rank > 0, 2, jnp.where(later > 0, 0, 1)))
    counts = [sum(jnp.where(kind == i, 1, 0) for kind in kinds) for i in range(2)]
    nexts = [jnp.int32(0), counts[0], counts[0] + counts[1]]
    for kind in kinds:
        places.append(jnp.where(kind == 0, nexts[0], jnp.where(kind == 1, nexts[1], nexts[2])))
        nexts = [at + jnp.where(kind == i, 1, 0) for i, at in enumerate(nexts)]
    return ranks, places


def chosen(tests, values):
    return sum(jnp.where(test, value, 0) for test, value in zip(tests, values))


class Root:
    def __init__(self, statistic, eye):
        width = statistic.shape[0]
        shift = total(jnp.where(eye, statistic, 0.0)) * (RIDGE / width)
        shifted = statistic + jnp.where(eye, shift, 0.0)
        scale = 2.5 / jnp.sqrt(total(shifted * shifted) + 1e-06)
        self.eye = eye
        self.gain = jnp.sqrt(jnp.sqrt(scale))
        self.power = scale * shifted
        self.next_factor()

    def next_factor(self):
        self.factor = split(jnp.where(self.eye, 1.25, 0.0) - 0.25 * self.power)


def kernel(
    side, own_ref, g_ref, ls_ref, rs_ref, upd_ref, ln_ref, rn_ref,
    parts, sums, second_sums, acc, picked0, picked1, grad0, grad1,
    left, right, left_out, right_out, ready0, ready1, home0, home1, lines0, lines1,
    block_at, owner_at, index_at, send_sum, recv_sum,
    send, recv, send_line, recv_line, local,
):
    n = side * side
    blocks = own_ref.shape[0]
    width = left.shape[1]
    me = lax.axis_index("dp")
    row, col = me // side, me % side
    chunk = HALF // 2
    picked, grad = (picked0, picked1), (grad0, grad1)
    ready, home, lines = (ready0, ready1), (home0, home1), (lines0, lines1)

    def peer(k):
        return ((row + k // side) % side) * side + (col + k % side) % side

    def along(axis, k):
        if axis == 0:
            return row * side + (col + k) % side
        return ((row + k) % side) * side + col

    core = lax.axis_index("shard") % 2

    def turned_round(i):
        return 1 + (i + me + core * (n // 2 - 1)) % (n - 1)

    loads = [
        pltpu.make_async_copy(ls_ref, left, local.at[1]),
        pltpu.make_async_copy(rs_ref, right, local.at[2]),
    ]
    pieces = [(j, kind) for j in range(2) for kind in range(2)]
    for j, kind in pieces:
        loads.append(
            pltpu.make_async_copy(
                g_ref.at[pl.ds(kind * HALF + j * chunk, chunk), (col, row)[kind]],
                parts.at[kind, j, 0],
                local.at[9 + 2 * j + kind],
            )
        )
    for load in loads:
        load.start()
    barrier = pltpu.get_barrier_semaphore()

    @pl.loop(1, n)
    def _(k):
        pl.semaphore_signal(barrier, inc=1, device_id={"dp": peer(k)}, device_id_type=MESH)

    def remote(src, dst, sent, landed, to):
        return pltpu.make_async_remote_copy(
            src_ref=src, dst_ref=dst, send_sem=sent, recv_sem=landed,
            device_id={"dp": to}, device_id_type=MESH,
        )

    def direct(what, half, k, src, dst):
        at = (2 * what + half, k)
        return remote(src, dst, send.at[at], recv.at[at], peer(k))

    def part_copy(j, kind, k):
        src = g_ref.at[pl.ds(kind * HALF + j * chunk, chunk), ((col, row)[kind] + k) % side]
        at = (0, kind, j, k)
        return remote(
            src, parts.at[kind, j, k], send_sum.at[at], recv_sum.at[at], along(kind, k)
        )

    def sum_copy(j, kind, k):
        src = sums.at[kind, j, ((row, col)[kind] + k) % side]
        at = (1, kind, j, k)
        return remote(
            src, second_sums.at[kind, j, k], send_sum.at[at], recv_sum.at[at], along(1 - kind, k)
        )

    def slot_copy(half, k):
        return direct(1, half, k, picked[half].at[k], grad[half].at[me])

    def home_copy(half, k):
        return direct(2, half, k, ready[half].at[peer(k)], home[half].at[me])

    def line_copy(half, step, axis, k):
        at = (half, step, axis, k)
        held = lines[half].at[axis]
        if step == 0:
            src = dst = held.at[(col, row)[axis]]
            to = along(axis, k)
        else:
            src, dst, to = held, line_place(half, axis), along(1 - axis, k)
        return remote(src, dst, send_line.at[at], recv_line.at[at], to)

    def line_place(half, axis):
        return upd_ref.at[half, axis, (row, col)[axis]]

    pl.semaphore_wait(barrier, n - 1)

    for j in range(2):
        for i in FAR_FIRST:
            for kind in range(2):
                part_copy(j, kind, i).start()

    owners = [own_ref[b] for b in range(blocks)]
    ranks, places = ranks_of(owners)

    @pl.loop(0, blocks)
    def _(p):
        tests = [at == p for at in places]
        block_at[p] = chosen(tests, range(blocks))
        owner_at[p] = chosen(tests, owners)

    @pl.loop(0, n)
    def _(k):
        to = peer(k)
        for half in range(2):
            index = jnp.int32(0)
            for p in range(half * HALF, (half + 1) * HALF):
                index = jnp.where(owner_at[p] == to, block_at[p], index)
            index_at[half, k] = index

    def mine(half, slot):
        tests = []
        for owner, rank, at in zip(owners, ranks, places):
            inside = (at < HALF) if half == 0 else (at >= HALF)
            tests.append((owner == me) & inside & ((rank == 0) if slot == 0 else (rank > 0)))
        return chosen(tests, [1] * blocks) > 0

    for number, (j, kind) in enumerate(pieces):
        loads[2 + number].wait()
        for k in range(1, side):
            part_copy(j, kind, k).wait_recv()

        @pl.loop(0, side)
        def _(v):
            sums[kind, j, v] = sum(parts[kind, j, k, :, v].astype(F32) for k in range(side))

        for k in FAR_FIRST:
            sum_copy(j, kind, k).start()
    for j, kind in pieces:
        for k in range(1, side):
            sum_copy(j, kind, k).wait_recv()
        acc[pl.ds(kind * HALF + j * chunk, chunk)] = sums[kind, j, (row, col)[kind]] + (
            second_sums[kind, j, 1] + second_sums[kind, j, 2] + second_sums[kind, j, 3]
        )

    for half in range(2):
        @pl.loop(0, n - 1)
        def _(i):
            k = turned_round(i)
            picked[half][k] = acc[index_at[half, k]]
            slot_copy(half, k).start()

        grad[half][me] = acc[index_at[half, 0]]

    def low_mine(half):
        tests = []
        for owner, at in zip(owners[:HALF], places[:HALF]):
            tests.append((owner == me) & ((at < HALF) if half == 0 else (at >= HALF)))
        return chosen(tests, [1] * HALF) > 0

    eye = lax.broadcasted_iota(jnp.int32, (width, width), 0) == lax.broadcasted_iota(
        jnp.int32, (width, width), 1
    )

    def solve(half, used, left_old, right_old, beside):
        @pl.loop(1, n)
        def _(k):
            slot_copy(half, k).wait_recv()

        across = jnp.stack([grad[half][(i % side) * side + i // side] for i in range(n)])
        value = jnp.where(low_mine(half), across, grad[half][...]).reshape(width, width)
        value = jnp.where(used, value, 0.0)
        plain, turned = split(value), split(value.T)
        left_new = DECAY * left_old + (1.0 - DECAY) * product(plain, turned)
        right_new = DECAY * right_old + (1.0 - DECAY) * product(turned, plain)
        if half == 0:
            left_out[0] = left_new
            right_out[0] = right_new
        else:
            for slot in range(2):
                here = mine(1, slot)
                for out, old, new in (
                    (left_out, left, left_new), (right_out, right, right_new)
                ):
                    rest = out[0] if slot == 0 else DECAY * old[1]
                    out[slot] = jnp.where(here, new, rest)
        count = 1.0 / (width * width)
        size = jnp.sqrt(total(value * value) * count)
        first, second = roots = Root(left_new, eye), Root(right_new, eye)
        moved = plain
        for step in range(1, ITERS):
            squares = [product(root.factor, root.factor) for root in roots]
            half_way = product(first.factor, moved)
            squares = [split(square) for square in squares]
            half_way = split(half_way)
            fourths = [product(square, square) for square in squares]
            moved = product(half_way, second.factor)
            fourths = [split(fourth) for fourth in fourths]
            powers = [split(root.power) for root in roots]
            moved = split(moved)
            for root, fourth, power in zip(roots, fourths, powers):
                root.power = product(fourth, power)
            for root in roots:
                root.next_factor()
            beside(step)
        moved = product(split(product(first.factor, moved)), second.factor)
        gain = first.gain * second.gain
        ratio = size / jnp.sqrt(gain * gain * total(moved * moved) * count + 1e-06)
        ready[half][...] = (moved * (gain * ratio)).astype(BF16).reshape(ready[half].shape)

        @pl.loop(0, n - 1)
        def _(i):
            home_copy(half, turned_round(i)).start()

        home[half][me] = ready[half][me]

    def along_first(half):
        @pl.loop(1, n)
        def _(k):
            home_copy(half, k).wait_recv()

        for axis in range(2):
            for p in range(chunk):
                value = home[half][owner_at[half * HALF + axis * chunk + p]]
                lines[half][axis, (col, row)[axis], p] = value
        for k in FAR_FIRST:
            for axis in range(2):
                line_copy(half, 0, axis, k).start()

    rests = []

    def along_second(half):
        for axis in range(2):
            for k in range(1, side):
                line_copy(half, 0, axis, k).wait_recv()
        for k in FAR_FIRST:
            for axis in range(2):
                line_copy(half, 1, axis, k).start()
        for axis in range(2):
            rest = pltpu.make_async_copy(
                lines[half].at[axis], line_place(half, axis), local.at[5 + 2 * half + axis]
            )
            rest.start()
            rests.append(rest)

    loads[0].wait()
    loads[1].wait()

    def beside_second(step):
        if step == 3:
            along_first(0)

    solve(0, mine(0, 0), left[0], right[0], lambda step: None)
    slot = jnp.where(mine(1, 1), 1, 0)
    used = mine(1, 0) | mine(1, 1)
    solve(1, used, left[slot], right[slot], beside_second)
    along_second(0)
    for ref, out, at in ((left_out, ln_ref, 3), (right_out, rn_ref, 4)):
        rest = pltpu.make_async_copy(ref, out, local.at[at])
        rest.start()
        rests.append(rest)
    along_first(1)
    along_second(1)

    @pl.loop(1, n)
    def _(k):
        for half in range(2):
            slot_copy(half, k).wait_send()
            home_copy(half, k).wait_send()

    for j, kind in pieces:
        for k in range(1, side):
            part_copy(j, kind, k).wait_send()
            sum_copy(j, kind, k).wait_send()
    for half in range(2):
        for axis in range(2):
            for k in range(1, side):
                line_copy(half, 0, axis, k).wait_send()
                line_copy(half, 1, axis, k).wait()
    for rest in rests:
        rest.wait()


def order_kernel(
    own_ref, upd_ref, ln_ref, rn_ref, out_ref, lo_ref, ro_ref, upd, left, right, whole, into, out
):
    blocks = own_ref.shape[0]
    side, chunk = upd.shape[2], upd.shape[4]
    reads = [
        pltpu.make_async_copy(upd_ref.at[half, axis], upd.at[half, axis], into.at[2 * half + axis])
        for half in range(2)
        for axis in range(2)
    ]
    reads += [
        pltpu.make_async_copy(ln_ref, left, into.at[4]),
        pltpu.make_async_copy(rn_ref, right, into.at[5]),
    ]
    for read in reads:
        read.start()
    _, places = ranks_of([own_ref[b] for b in range(blocks)])
    writes = []
    for p in range(blocks):
        half, axis, i = p // HALF, p % HALF // chunk, p % chunk
        if i == 0:
            reads[2 * half + axis].wait()
        for row in range(side):
            for col in range(side):
                line, at = (row, col) if axis == 0 else (col, row)
                whole[p, row * side + col] = upd[half, axis, line, at, i]
        block = chosen([place == p for place in places], range(blocks))
        writes.append(pltpu.make_async_copy(whole.at[p], out_ref.at[block], out.at[p]))
        writes[-1].start()
    for i, ref, to in ((0, left, lo_ref), (1, right, ro_ref)):
        reads[4 + i].wait()
        writes.append(pltpu.make_async_copy(ref, to, out.at[blocks + i]))
        writes[-1].start()
    for write in writes:
        write.wait()


def local(side, grad_parts, owner_list, left_stats, right_stats):
    n = side * side
    _, blocks, width, _ = grad_parts.shape
    owners = owner_list[:, 0]
    tiles = (blocks, n, ROWS, width)
    pair = (2, width, width)
    vmem = pltpu.VMEM
    anywhere = pl.BlockSpec(memory_space=pl.ANY)
    scalars = pl.BlockSpec(memory_space=pltpu.SMEM)
    piece = (n, ROWS, width)
    gathered = (2, 2, side, side, HALF // 2, ROWS, width)
    shapes = (
        jax.ShapeDtypeStruct(gathered, BF16),
        jax.ShapeDtypeStruct(pair, F32),
        jax.ShapeDtypeStruct(pair, F32),
    )
    dma = pltpu.SemaphoreType.DMA
    update, left_new, right_new = pl.pallas_call(
        functools.partial(kernel, side),
        out_shape=shapes,
        in_specs=[scalars] + [anywhere] * 3,
        out_specs=(anywhere,) * 3,
        scratch_shapes=[
            vmem((2, 2, side, HALF // 2, side, ROWS, width), BF16),
            vmem((2, 2, side, HALF // 2, ROWS, width), F32),
            vmem((2, 2, side, HALF // 2, ROWS, width), F32),
            vmem((blocks, ROWS, width), F32),
        ]
        + [vmem(piece, F32)] * 4
        + [vmem(pair, F32)] * 4
        + [vmem(piece, BF16)] * 4
        + [vmem((2, side, HALF // 2, ROWS, width), BF16)] * 2
        + [
            pltpu.SMEM((blocks,), jnp.int32),
            pltpu.SMEM((blocks,), jnp.int32),
            pltpu.SMEM((2, n), jnp.int32),
            dma((2, 2, 2, side)),
            dma((2, 2, 2, side)),
            dma((6, n)),
            dma((6, n)),
            dma((2, 2, 2, side)),
            dma((2, 2, 2, side)),
            dma((13,)),
        ],
        compiler_params=pltpu.CompilerParams(
            collective_id=0, has_side_effects=True, vmem_limit_bytes=VMEM_BYTES
        ),
    )(
        owners,
        grad_parts.reshape(blocks, side, side, ROWS, width),
        left_stats.reshape(pair),
        right_stats.reshape(pair),
    )
    update, left_new, right_new = pl.pallas_call(
        order_kernel,
        out_shape=(jax.ShapeDtypeStruct(tiles, BF16),) + shapes[1:],
        in_specs=[scalars] + [anywhere] * 3,
        out_specs=(anywhere,) * 3,
        scratch_shapes=[
            vmem(gathered, BF16),
            vmem(pair, F32),
            vmem(pair, F32),
            vmem(tiles, BF16),
            dma((6,)),
            dma((blocks + 2,)),
        ],
        compiler_params=pltpu.CompilerParams(vmem_limit_bytes=VMEM_BYTES),
    )(owners, update, left_new, right_new)
    return (
        update.reshape(blocks, width, width),
        left_new.reshape(left_stats.shape),
        right_new.reshape(right_stats.shape),
    )


def solution(mesh):
    side = int(round(mesh.shape["dp"] ** 0.5))
    return jax.shard_map(
        functools.partial(local, side),
        mesh=mesh,
        in_specs=(
            P("dp", "shard", None, None),
            P("shard", None),
            P("dp", "shard", None, None, None),
            P("dp", "shard", None, None, None),
        ),
        out_specs=(
            P("shard", None, None),
            P("dp", "shard", None, None, None),
            P("dp", "shard", None, None, None),
        ),
        check_vma=False,
    )
```
